256 devices in a mesh: query: 32 (over x, z), owner: 2 (over core), tensor: 4 (over y).
Axes of the slice: x: 4, y: 4, z: 8, core: 2. Of those that a mesh axis runs over, the one named last changes fastest.
Arguments:
- patches: bfloat16 [32, 2, 8, 257, 1408], P('query', 'owner'), may hold values from -64 to 64
- states: bfloat16 [2048, 32, 768], P(('query', 'owner')), may hold values from -64 to 64
- pair_source: int32 [2048, 1], P(('query', 'owner')), may hold values from 0 to 31; in each aligned block of 32 rows (0 to 31, 32 to 63, ...) at most 2 rows name the same one
- pair_image: int32 [2048], P(('query', 'owner')), may hold values from 0 to 7
- w_query: bfloat16 [768, 768], P(None, 'tensor'), may hold values from -0.21875 to 0.21875
- w_key: bfloat16 [1408, 768], P(None, 'tensor'), may hold values from -0.15625 to 0.15625
- w_value: bfloat16 [1408, 768], P(None, 'tensor'), may hold values from -0.15625 to 0.15625
- w_out: bfloat16 [768, 768], P('tensor'), may hold values from -0.21875 to 0.21875
- w_in: bfloat16 [768, 3072], P(None, 'tensor'), may hold values from -1 to 1
- w_down: bfloat16 [3072, 768], P('tensor'), may hold values from -2 to 2
- w_match: bfloat16 [768], replicated, may hold values from -1.25 to 1.25
Outputs:
- rankings: float32 [32, 64], P(None, 'owner')
The draws below stay inside these ranges and needn't reach their ends.
Inputs may be any that keep to these rules, and one draw needn't show every extreme that they name: `pair_source`: among the pairs of one device no query index appears more than 2 times, and it appears exactly 2 times on some device.
All inputs are finite; a program needn't handle non-finite values.
Results may differ from the reference program's by a relative error of at most 0.0015.
Values may be sent and summed in bfloat16 or wider, within the bound.
A program may use at most 128 MiB of HBM per device.

```python
import math
import jax
import jax.numpy as jnp
import numpy as np
from jax import lax

D = 768
HEADS = 12
HEAD_SIZE = 64
FF = 3072
VIS = 1408
NQ = 32
PATCH = 257
PAIR_DEV = 32
IMG_DEV = 8
CAP = 2
PAIRS = 2048
N_QUERY = 32
N_OWNER = 2
N_TENSOR = 4


def draw_patches(key, part):
    key = jax.random.fold_in(key, 17)
    base_key = jax.random.fold_in(key, 0)
    leading = (N_QUERY, N_OWNER, IMG_DEV)
    field = jnp.clip(jax.random.normal(base_key, leading + (PATCH, VIS), jnp.float32), -6.0, 6.0)
    return field.astype(jnp.bfloat16)


def draw_states(key, part):
    key = jax.random.fold_in(key, 23)
    base_key = jax.random.fold_in(key, 0)
    total_pairs = N_QUERY * N_OWNER * PAIR_DEV
    field = jnp.clip(jax.random.normal(base_key, (total_pairs, NQ, D), jnp.float32), -6.0, 6.0)
    return field.astype(jnp.bfloat16)


def draw_w_in(key, part):
    key = jax.random.fold_in(key, 37)
    common_key, own_key = jax.random.split(key, 2)
    common = jnp.clip(jax.random.normal(common_key, (D, 1), jnp.float32), -4.0, 4.0)
    own = jnp.clip(jax.random.normal(own_key, (D, FF), jnp.float32), -4.0, 4.0)
    shared_part = 0.5
    own_part = 0.866
    field = D ** (-0.5) * (shared_part * common + own_part * own)
    return field.astype(jnp.bfloat16)


def draw_w_down(key, part):
    key = jax.random.fold_in(key, 41)
    common_key, own_key = jax.random.split(key, 2)
    block_rows = FF // N_TENSOR
    common = jnp.clip(jax.random.normal(common_key, (1, block_rows, D), jnp.float32), -4.0, 4.0)
    own = jnp.clip(jax.random.normal(own_key, (N_TENSOR, block_rows, D), jnp.float32), -4.0, 4.0)
    shared_part = 0.9
    own_part = 0.44
    field = 2.5 * FF ** (-0.5) * (shared_part * common + own_part * own)
    return field.reshape(FF, D).astype(jnp.bfloat16)


def plant(array, key, low, largest):
    spot = [jax.random.randint(jax.random.fold_in(key, axis), (), 0, length) for axis, length in enumerate(array.shape)]
    longest = array.shape.index(max(array.shape))
    beside = spot[:longest] + [(spot[longest] + 1) % array.shape[longest]] + spot[longest + 1:]
    return array.at[tuple(spot)].set(low).at[tuple(beside)].set(largest)


def steps_of(rng, dims, pieces, least, high):
    level, own = 1.0, jax.random.fold_in(rng, 6)
    for axis_at, shards_of in pieces:
        heights = jnp.exp(jax.random.uniform(jax.random.fold_in(own, axis_at), (shards_of,), jnp.float32, least / len(pieces), high / len(pieces)))
        level = level * jnp.repeat(heights, dims[axis_at] // shards_of).reshape([-1 if axis == axis_at else 1 for axis in range(len(dims))])
    return level


def assign_block(key, own, number, rows, number_of, top, bound, slope):
    sequence = jax.random.permutation(key, number_of)
    heavy_load, usual = portions_of(number_of, rows * top, bound, slope, True), portions_of(number_of, rows * top, bound, slope, False)
    places = jnp.arange(number_of)

    def named(lengths, rotation):
        used = int((lengths > 0).sum())
        fixed = max(1, used // 4)
        shifted = fixed + (places - fixed + rotation * (used - fixed)) % max(1, number_of - fixed)
        return jnp.zeros((number_of,), jnp.int32).at[sequence[jnp.where(places < fixed, places, shifted)]].set(jnp.asarray(lengths, jnp.int32))

    lengths = jnp.where(number % 4 == 0, named(heavy_load, number // 4), named(usual, number - number // 4 - 1))
    mixed = jax.random.permutation(jax.random.fold_in(own, 3), number_of)
    giver, receiver = mixed[0:number_of // 2 * 2:2], mixed[1:number_of // 2 * 2:2]
    slack = jnp.minimum(lengths[giver] - 1, bound - lengths[receiver]) // 2
    slack = jnp.where((giver == sequence[0]) | (receiver == sequence[0]) | (lengths[receiver] == 0), 0, jnp.maximum(slack, 0))
    shifted = jax.random.randint(jax.random.fold_in(own, 4), (number_of // 2,), 0, 1 << 20) % (slack + 1)
    lengths = lengths.at[giver].add(-shifted).at[receiver].add(shifted)
    items = jnp.searchsorted(jnp.cumsum(lengths), jnp.arange(rows * top), side="right").astype(jnp.int32)
    table = items.reshape(top, rows).T
    table = table[jax.random.permutation(jax.random.fold_in(own, 1), rows)]
    rotation = jax.random.randint(jax.random.fold_in(own, 2), (rows, 1), 0, top)
    return jnp.take_along_axis(table, (jnp.arange(top)[None, :] + rotation) % top, axis=1)


def portions_of(count, total, reach, slope, full):
    weights = [(1 << 20) // math.isqrt(rank ** slope) + 1 for rank in range(1, count + 1)]
    largest = reach if full else min(reach, max(-(-total // count), total * weights[0] // sum(weights)))
    least = 1 if total - largest >= count - 1 else 0
    holding, surplus = [largest] + [least] * (count - 1), total - largest - least * (count - 1)
    while surplus > 0:
        candidates = [i for i in range(1, count) if holding[i] < largest] or [i for i in range(1, count) if holding[i] < reach]
        whole, left = sum([weights[i] for i in candidates]), surplus
        for i in candidates:
            extra = min(reach - holding[i], max(1, left * weights[i] // whole), surplus)
            holding[i] = holding[i] + extra
            surplus = surplus - extra
    return np.array(holding)


def noise(stream_key, shape, scale, most, cuts=(), kind=jnp.bfloat16):
    gain = steps_of(stream_key, shape, cuts, -0.22, 0.18) if cuts else 1.0
    drawn = jax.random.normal(stream_key, shape, jnp.float32) * scale * gain
    return jnp.minimum(jnp.maximum(drawn, -most), most).astype(kind)


def setup_inputs(seed: int = 0) -> dict:
    splits = jax.random.split(jax.random.key(seed), 12)
    patches = draw_patches(jax.random.fold_in(splits[11], 71), 0)
    states = draw_states(jax.random.fold_in(splits[11], 71), 0)
    pair_source_keys = jax.random.split(jax.random.fold_in(splits[2], 1), PAIRS // PAIR_DEV)
    pair_source_turns = jax.random.permutation(jax.random.fold_in(splits[2], 3), PAIRS // PAIR_DEV)
    pair_source = jax.vmap(lambda own, number: assign_block(jax.random.fold_in(splits[2], 2), own, number, PAIR_DEV, N_QUERY, 1, CAP, 2))(pair_source_keys, pair_source_turns).reshape((PAIRS, 1))
    pair_image = plant(jax.random.randint(splits[3], (PAIRS,), 0, IMG_DEV), jax.random.fold_in(splits[3], 1), 0, IMG_DEV - 1).astype(jnp.int32)
    w_query = noise(splits[4], (D, D), D ** -0.5, 0.21875, ((1, 4),))
    w_key = noise(splits[5], (VIS, D), VIS ** -0.5, 0.15625, ((1, 4),))
    w_value = noise(splits[6], (VIS, D), VIS ** -0.5, 0.15625, ((1, 4),))
    w_out = noise(splits[7], (D, D), D ** -0.5, 0.21875, ((0, 4),))
    w_in = draw_w_in(jax.random.fold_in(splits[11], 71), 0)
    w_down = draw_w_down(jax.random.fold_in(splits[11], 71), 0)
    w_match = noise(splits[10], (D,), 25 ** -0.5, 1.25)
    return dict(patches=patches, states=states, pair_source=pair_source, pair_image=pair_image, w_query=w_query, w_key=w_key, w_value=w_value, w_out=w_out, w_in=w_in, w_down=w_down, w_match=w_match)


EPSILON = 1e-06

def layer_norm(blended):
    average = lax.optimization_barrier(jnp.mean(blended, axis=-1, keepdims=True))
    squares = lax.optimization_barrier(jnp.mean(blended * blended, axis=-1, keepdims=True))
    return (blended - average) * lax.rsqrt(squares - average * average + EPSILON)

def attend_all(query_rows, key_rows, value_rows):
    pair_count = query_rows.shape[0]
    split_q = query_rows.astype(jnp.float32).reshape(pair_count, NQ, HEADS, HEAD_SIZE)
    split_k = key_rows.astype(jnp.float32).reshape(pair_count, PATCH, HEADS, HEAD_SIZE)
    split_v = value_rows.astype(jnp.float32).reshape(pair_count, PATCH, HEADS, HEAD_SIZE)
    scores = jnp.einsum('bqhd,bkhd->bhqk', split_q, split_k) * HEAD_SIZE ** (-0.5)
    highest = lax.optimization_barrier(jnp.max(scores, axis=-1, keepdims=True))
    raised = jnp.exp(scores - highest)
    weights = (raised / lax.optimization_barrier(jnp.sum(raised, axis=-1, keepdims=True))).astype(jnp.bfloat16)
    context = jnp.einsum('bhqk,bkhd->bqhd', weights.astype(jnp.float32), split_v)
    return context.astype(jnp.bfloat16).reshape(pair_count, NQ, D)

def reference(patches, states, pair_source, pair_image, w_query, w_key, w_value, w_out, w_in, w_down, w_match):
    images_flat = patches.reshape(N_QUERY * N_OWNER * IMG_DEV, PATCH, VIS)

    def project(image):
        key_part = jnp.dot(image, w_key, preferred_element_type=jnp.float32).astype(jnp.bfloat16)
        value_part = jnp.dot(image, w_value, preferred_element_type=jnp.float32).astype(jnp.bfloat16)
        return (key_part, value_part)
    key_all, value_all = lax.map(project, images_flat)
    group_count = N_QUERY * N_OWNER
    grouped = states.reshape(group_count, PAIR_DEV, NQ, D)
    owner_index = (jnp.arange(group_count, dtype=jnp.int32) % N_OWNER).astype(jnp.int32)
    sources = pair_source[:, 0].reshape(group_count, PAIR_DEV).astype(jnp.int32)
    locals_index = pair_image.reshape(group_count, PAIR_DEV).astype(jnp.int32)
    image_ids = ((sources * N_OWNER + owner_index[:, None]) * IMG_DEV + locals_index).astype(jnp.int32)
    match_dir = w_match.astype(jnp.float32)

    def one_group(inputs):
        tokens, chosen_ids = inputs
        query_rows = jnp.dot(tokens, w_query, preferred_element_type=jnp.float32).astype(jnp.bfloat16)
        context = attend_all(query_rows, key_all[chosen_ids], value_all[chosen_ids])
        attended = jnp.dot(context, w_out, preferred_element_type=jnp.float32)
        first_norm = layer_norm(tokens.astype(jnp.float32) + attended).astype(jnp.bfloat16)
        up_proj = jnp.dot(first_norm, w_in, preferred_element_type=jnp.float32)
        hidden = jax.nn.gelu(up_proj, approximate=False).astype(jnp.bfloat16)
        fed = jnp.dot(hidden, w_down, preferred_element_type=jnp.float32)
        second_norm = layer_norm(first_norm.astype(jnp.float32) + fed)
        return lax.optimization_barrier(jnp.mean(lax.optimization_barrier(jnp.sum(second_norm * match_dir, axis=-1)), axis=1))
    match_score = lax.map(one_group, (grouped, image_ids)).reshape(N_QUERY, N_OWNER * PAIR_DEV)
    partition = lax.optimization_barrier(jnp.sum(jnp.exp(match_score), axis=1, keepdims=True))
    return match_score - jnp.log(partition)
```

```python
import functools

import jax
import jax.numpy as jnp
from jax import lax
from jax.experimental import pallas as pl
from jax.experimental.pallas import tpu as pltpu
from jax.sharding import PartitionSpec as P

D = 768
PATCH = 257
VIS = 1408
PAIRS = 32
NQ = 32
IMAGES = 8
SLOTS = 2
NX, NZ = 4, 8
GROUPS = NX * NZ
TENSOR = 4
PACK = 48
KEYS = 384
ROWS = PAIRS // TENSOR * NQ
EPSILON = 1e-06
MESH = pl.DeviceIdType.MESH
bf16, f32 = jnp.bfloat16, jnp.float32


def kernel(
    idx, img, states_h, patches_h, wq_h, wk_h, wv_h, wout_h, win_h, wdn_h, match_ref,
    out_ref,
    states, patches, wq, wk, wv, wqx, wkvx,
    qpk, qsend, qrecv, csend, crecv, keys, values, img_recv, img_s,
    ysend, yrecv, wout, win, wdn, fsend, frecv, ssend, srecv, osend, orecv,
    load_sem, img_ss, img_rs, q_ss, q_rs, c_ss, c_rs, y_ss, y_rs,
    w_own, w_ss, w_rs, f_ss, f_rs, s_ss, s_rs, o_ss, o_rs, img_sem,
):
    me = lax.axis_index("query")
    core = lax.axis_index("owner")
    ty = lax.axis_index("tensor")
    x, z = me // NZ, me % NZ

    def peer(k):
        iz, ix = k // NX, k % NX
        dz = ((iz + 1) // 2) * (2 * (iz % 2) - 1)
        dx = ((ix + 1) // 2) * (2 * (ix % 2) - 1)
        return ((x + dx + NX) % NX) * NZ + (z + dz + NZ) % NZ

    def y_peer(k):
        return (ty + k) % TENSOR

    def remote(src, dst, ss, rs, **device):
        return pltpu.make_async_remote_copy(
            src_ref=src, dst_ref=dst, send_sem=ss, recv_sem=rs, device_id=device, device_id_type=MESH
        )

    loads = [
        pltpu.make_async_copy(src, dst, load_sem.at[i])
        for i, (src, dst) in enumerate(
            ((states_h, states), (wq_h, wq), (wk_h, wk), (wv_h, wv), (patches_h.at[0, 0], patches))
        )
    ]
    for copy in loads:
        copy.start()

    barrier = pltpu.get_barrier_semaphore()

    @pl.loop(1, GROUPS)
    def _(k):
        pl.semaphore_signal(barrier, inc=1, device_id={"query": peer(k)}, device_id_type=MESH)

    for k in range(1, TENSOR):
        pl.semaphore_signal(barrier, inc=1, device_id={"tensor": y_peer(k)}, device_id_type=MESH)
    pl.semaphore_signal(barrier, inc=1, device_id={"owner": 1 - core}, device_id_type=MESH)

    loads[0].wait()
    loads[1].wait()
    w = wq[...]
    wqx[...] = jnp.concatenate([w, w[:, 128:]], axis=1)
    low = lax.broadcasted_iota(jnp.int32, (1, 128), 1) < 64

    @pl.loop(0, PAIRS // 4)
    def _(b):
        rows = states[pl.ds(b * 4, 4)].reshape(4 * NQ, D)
        q = jnp.dot(rows, wqx[...], preferred_element_type=f32).reshape(4, NQ, 256)
        first, second = q[:, :, :128], q[:, :, 128:]
        last = jnp.where(low[None], second[:, :16], second[:, 16:])
        qpk[pl.ds(b * 4, 4)] = jnp.concatenate([first, last], axis=1).astype(bf16)

    pl.semaphore_wait(barrier, GROUPS + TENSOR - 1)

    def img_copy(dst, src):
        return remote(img.at[dst], img_recv.at[src], img_ss.at[dst], img_rs.at[src], query=dst)

    @pl.loop(1, GROUPS)
    def _(k):
        img_copy(peer(k), me).start()

    def of(ref, p):
        return ref.at[pl.ds(p * SLOTS, SLOTS)]

    def q_copy(dst, src):
        return remote(of(qsend, dst), of(qrecv, src), q_ss.at[dst], q_rs.at[src], query=dst)

    def c_copy(dst, src):
        return remote(of(csend, dst), of(crecv, src), c_ss.at[dst], c_rs.at[src], query=dst)

    @pl.loop(0, GROUPS)
    def _(k):
        p = peer(k)
        for s in range(SLOTS):
            qsend[p * SLOTS + s] = qpk[idx[p * SLOTS + s]]

        @pl.when(k > 0)
        def _():
            q_copy(p, me).start()

    right, left, across = y_peer(1), y_peer(3), y_peer(2)
    shards = ((wout_h, wout, 192), (win_h, win, D), (wdn_h, wdn, D))

    def part(ref, t, size, begin, length):
        return ref.at[t, pl.ds(begin, length)]

    def own(i):
        src, dst, size = shards[i]
        return pltpu.make_async_copy(src, dst.at[ty, pl.ds(0, size)], w_own.at[i])

    def first_hop(i, to_right):
        src, dst, size = shards[i]
        begin = pl.multiple_of(core * (size // 2), size // 2)
        j = 0 if to_right else 1
        return remote(
            src.at[pl.ds(begin, size // 2)], dst.at[ty, pl.ds(begin, size // 2)],
            w_ss.at[i, j], w_rs.at[i, j], tensor=right if to_right else left,
        )

    def second_hop(i, to_right, receive=False):
        _, dst, size = shards[i]
        quarter = size // 4
        t = across if receive else (left if to_right else right)
        begin = pl.multiple_of(core * (size // 2) + (0 if to_right else quarter), quarter)
        place = dst.at[t, pl.ds(begin, quarter)]
        j = 2 if to_right else 3
        return remote(place, place, w_ss.at[i, j], w_rs.at[i, j], tensor=right if to_right else left)

    def sibling(i, which, receive=False):
        _, dst, size = shards[i]
        c = 1 - core if receive else core
        quarter = size // 4
        if which < 2:
            t, begin, length = (left if which == 0 else right), c * (size // 2), size // 2
        else:
            t, begin, length = across, c * (size // 2) + (which - 2) * quarter, quarter
        place = dst.at[t, pl.ds(pl.multiple_of(begin, quarter), length)]
        return remote(place, place, w_ss.at[i, 4 + which], w_rs.at[i, 4 + which], owner=1 - core)

    def weights_0(i):
        own(i).start()
        first_hop(i, True).start()
        first_hop(i, False).start()

    def weights_1(i):
        first_hop(i, True).wait_recv()
        second_hop(i, True).start()
        sibling(i, 0).start()
        first_hop(i, False).wait_recv()
        second_hop(i, False).start()
        sibling(i, 1).start()

    def weights_2(i):
        second_hop(i, True, True).wait_recv()
        sibling(i, 2).start()
        second_hop(i, False, True).wait_recv()
        sibling(i, 3).start()

    def weights_3(i):
        for which in range(4):
            sibling(i, which, True).wait_recv()
        own(i).wait()

    for i in range(3):
        weights_0(i)

    for copy in loads[2:]:
        copy.wait()
    w = wk[...]
    wkvx[:, :256] = jnp.concatenate([w, w[:, 128:]], axis=1)
    w = wv[...]
    wkvx[:, 256:] = jnp.concatenate([w, w[:, 128:]], axis=1)

    @pl.loop(0, IMAGES)
    def _(i):
        both = jnp.dot(patches[i], wkvx[...], preferred_element_type=f32).astype(bf16)
        pad = jnp.zeros((KEYS - 256, 256), bf16)
        keys[i, 256:KEYS] = pad
        values[i, 256:KEYS] = pad
        keys[i, 0:PATCH] = both[:, :256]
        values[i, 0:PATCH] = both[:, 256:]

    img_recv[me] = img[me]

    @pl.loop(1, GROUPS)
    def _(k):
        p = peer(k)
        img_copy(p, p).wait_recv()

    to_scalars = pltpu.make_async_copy(img_recv, img_s, img_sem)
    to_scalars.start()
    to_scalars.wait()

    first_mask = low.astype(f32).astype(bf16)
    second_mask = (1 - low.astype(f32)).astype(bf16)
    column = lax.broadcasted_iota(jnp.int32, (1, KEYS), 1)

    def attend(rows, image):
        a, b = rows[0:32], rows[32:48]
        top = jnp.concatenate([a * first_mask, a * second_mask, jnp.zeros((32, 128), bf16)], axis=0)
        bottom = jnp.concatenate([jnp.zeros((64, 128), bf16), b * first_mask, b * second_mask], axis=0)
        q = jnp.concatenate([top, bottom], axis=1)
        scores = lax.dot_general(q, keys[image], (((1,), (1,)), ((), ())), preferred_element_type=f32)
        scores = jnp.where(column < PATCH, scores * 0.125, -jnp.inf)
        raised = jnp.exp(scores - jnp.max(scores, axis=1, keepdims=True))
        weights = (raised / jnp.sum(raised, axis=1, keepdims=True)).astype(bf16)
        c = jnp.dot(weights, values[image], preferred_element_type=f32)
        c01 = jnp.where(low, c[0:32, :128], c[32:64, :128])
        c2 = jnp.where(low, c[64:80, 128:], c[80:96, 128:])
        return jnp.concatenate([c01, c2], axis=0).astype(bf16)

    qrecv[pl.ds(me * SLOTS, SLOTS)] = qsend[pl.ds(me * SLOTS, SLOTS)]

    @pl.loop(0, GROUPS)
    def _(k):
        p = peer(k)

        @pl.when(k > 0)
        def _():
            q_copy(p, p).wait_recv()

        done = [attend(qrecv[p * SLOTS + s], img_s[p, 0, s]) for s in range(SLOTS)]
        for s in range(SLOTS):
            csend[p * SLOTS + s] = done[s]

        @pl.when(k > 0)
        def _():
            c_copy(p, me).start()

    for i in range(3):
        weights_1(i)

    crecv[pl.ds(me * SLOTS, SLOTS)] = csend[pl.ds(me * SLOTS, SLOTS)]

    @pl.loop(1, GROUPS)
    def _(k):
        p = peer(k)
        c_copy(p, p).wait_recv()

    @pl.loop(0, PAIRS)
    def _(j):
        ysend[j // 8, j % 8] = crecv[idx[GROUPS * SLOTS + j]]

    def y_copy(dst, src):
        return remote(ysend.at[dst], yrecv.at[src], y_ss.at[dst], y_rs.at[src], tensor=dst)

    for k in range(1, TENSOR):
        y_copy(y_peer(k), ty).start()
    yrecv[ty] = ysend[ty]

    for i in range(3):
        weights_2(i)
    weights_3(0)
    for t in range(TENSOR):
        wout[t, 192:256] = wout[t, 128:192]
    for k in range(1, TENSOR):
        t = y_peer(k)
        y_copy(t, t).wait_recv()

    def norm(v):
        mean = jnp.mean(v, axis=-1, keepdims=True)
        squares = jnp.mean(v * v, axis=-1, keepdims=True)
        return (v - mean) * lax.rsqrt(squares - mean * mean + EPSILON)

    total = states[pl.ds(ty * 8, 8)].reshape(ROWS, D).astype(f32)
    for t in range(TENSOR):
        c = yrecv[t]
        b = c[:, 32:]
        second = jnp.concatenate([b * first_mask[None], b * second_mask[None]], axis=1)
        rows = jnp.concatenate([c[:, :32], second], axis=2).reshape(ROWS, 256)
        total = total + jnp.dot(rows, wout[t], preferred_element_type=f32)
    first_norm = norm(total).astype(bf16)

    for i in (1, 2):
        weights_3(i)
    total = first_norm.astype(f32)
    for t in range(TENSOR):
        for n in range(0, D, 256):
            up = jnp.dot(first_norm, win[t, :, n : n + 256], preferred_element_type=f32)
            hidden = (0.5 * up * (1.0 + lax.erf(up * 0.7071067811865476))).astype(bf16)
            total = total + jnp.dot(hidden, wdn[t, n : n + 256, :], preferred_element_type=f32)
    score = jnp.sum(norm(total) * match_ref[...].astype(f32), axis=-1, keepdims=True)
    score = jnp.mean(score.reshape(8, NQ, 1), axis=1)

    lane = lax.broadcasted_iota(jnp.int32, (8, 128), 1)
    pair = lax.broadcasted_iota(jnp.int32, (8, 128), 0) + (core * PAIRS + ty * 8)
    row = jnp.sum(jnp.where(lane == pair, score, 0.0), axis=0, keepdims=True)
    fsend[...] = row

    def f_copy(dst, src):
        return remote(fsend, frecv.at[src], f_ss.at[dst], f_rs.at[src], tensor=dst)

    for k in range(1, TENSOR):
        f_copy(y_peer(k), ty).start()
    frecv[ty] = row
    for k in range(1, TENSOR):
        t = y_peer(k)
        f_copy(t, t).wait_recv()
    row = frecv[0] + frecv[1] + frecv[2] + frecv[3]
    ssend[...] = row
    s_copy = remote(ssend, srecv, s_ss, s_rs, owner=1 - core)
    s_copy.start()
    s_copy.wait_recv()
    row = row + srecv[...]
    valid = lax.broadcasted_iota(jnp.int32, (1, 128), 1) < 2 * PAIRS
    partition = jnp.sum(jnp.where(valid, jnp.exp(row), 0.0), axis=1, keepdims=True)
    row = row - jnp.log(partition)
    row = jnp.where(core == 0, row, pltpu.roll(row, 128 - PAIRS, 1))
    osend[...] = row
    orecv[me] = row

    def o_copy(dst, src):
        return remote(osend, orecv.at[src], o_ss.at[dst], o_rs.at[src], query=dst)

    @pl.loop(1, GROUPS)
    def _(k):
        o_copy(peer(k), me).start()

    @pl.loop(1, GROUPS)
    def _(k):
        p = peer(k)
        o_copy(p, p).wait_recv()

    out_ref[...] = orecv[...].reshape(GROUPS, 128)[:, :PAIRS]

    @pl.loop(1, GROUPS)
    def _(k):
        p = peer(k)
        img_copy(p, p).wait_send()
        q_copy(p, p).wait_send()
        c_copy(p, p).wait_send()
        o_copy(p, p).wait_send()

    for k in range(1, TENSOR):
        t = y_peer(k)
        y_copy(t, t).wait_send()
        f_copy(t, t).wait_send()
    s_copy.wait_send()
    for i in range(3):
        first_hop(i, True).wait_send()
        first_hop(i, False).wait_send()
        second_hop(i, True).wait_send()
        second_hop(i, False).wait_send()
        for which in range(4):
            sibling(i, which).wait_send()


def body(
    patches, states, pair_source, pair_image, w_query, w_key, w_value, w_out, w_in, w_down, w_match
):
    source = pair_source[:, 0]
    number = jnp.arange(PAIRS, dtype=jnp.int32)
    earlier = (source[:, None] == source[None, :]) & (number[None, :] < number[:, None])
    slot_of = source * SLOTS + jnp.sum(earlier.astype(jnp.int32), axis=1)
    placed = slot_of[None, :] == jnp.arange(GROUPS * SLOTS, dtype=jnp.int32)[:, None]
    pair_of = jnp.sum(jnp.where(placed, number[None, :], 0), axis=1)
    idx = jnp.concatenate([pair_of, slot_of, jnp.zeros((32,), jnp.int32)])
    lanes = jnp.arange(128, dtype=jnp.int32)
    at = jnp.where(lanes < SLOTS, jnp.arange(GROUPS, dtype=jnp.int32)[:, None] * SLOTS + lanes, -1)
    img = jnp.sum(jnp.where(at[:, :, None] == slot_of, pair_image, 0), axis=2).reshape(GROUPS, 1, 128)

    vmem = pl.BlockSpec(memory_space=pltpu.VMEM)
    hbm = pl.BlockSpec(memory_space=pl.ANY)
    dma = pltpu.SemaphoreType.DMA
    return pl.pallas_call(
        kernel,
        out_shape=jax.ShapeDtypeStruct((GROUPS, PAIRS), f32),
        in_specs=[pl.BlockSpec(memory_space=pltpu.SMEM), vmem] + [hbm] * 8 + [vmem],
        out_specs=vmem,
        scratch_shapes=[
            pltpu.VMEM((PAIRS, NQ, D), bf16),
            pltpu.VMEM((IMAGES, PATCH, VIS), bf16),
            pltpu.VMEM((D, 192), bf16),
            pltpu.VMEM((VIS, 192), bf16),
            pltpu.VMEM((VIS, 192), bf16),
            pltpu.VMEM((D, 256), bf16),
            pltpu.VMEM((VIS, 512), bf16),
            pltpu.VMEM((PAIRS, PACK, 128), bf16),
            pltpu.VMEM((GROUPS * SLOTS, PACK, 128), bf16),
            pltpu.VMEM((GROUPS * SLOTS, PACK, 128), bf16),
            pltpu.VMEM((GROUPS * SLOTS, PACK, 128), bf16),
            pltpu.VMEM((GROUPS * SLOTS, PACK, 128), bf16),
            pltpu.VMEM((IMAGES, KEYS, 256), bf16),
            pltpu.VMEM((IMAGES, KEYS, 256), bf16),
            pltpu.VMEM((GROUPS, 1, 128), jnp.int32),
            pltpu.SMEM((GROUPS, 1, 128), jnp.int32),
            pltpu.VMEM((TENSOR, 8, PACK, 128), bf16),
            pltpu.VMEM((TENSOR, 8, PACK, 128), bf16),
            pltpu.VMEM((TENSOR, 256, D), bf16),
            pltpu.VMEM((TENSOR, D, D), bf16),
            pltpu.VMEM((TENSOR, D, D), bf16),
            pltpu.VMEM((1, 128), f32),
            pltpu.VMEM((TENSOR, 1, 128), f32),
            pltpu.VMEM((1, 128), f32),
            pltpu.VMEM((1, 128), f32),
            pltpu.VMEM((1, 128), f32),
            pltpu.VMEM((GROUPS, 1, 128), f32),
            dma((5,)),
            dma((GROUPS,)), dma((GROUPS,)),
            dma((GROUPS,)), dma((GROUPS,)),
            dma((GROUPS,)), dma((GROUPS,)),
            dma((TENSOR,)), dma((TENSOR,)),
            dma((3,)), dma((3, 8)), dma((3, 8)),
            dma((TENSOR,)), dma((TENSOR,)),
            dma, dma,
            dma((GROUPS,)), dma((GROUPS,)),
            dma,
        ],
        compiler_params=pltpu.CompilerParams(
            collective_id=0, has_side_effects=True, vmem_limit_bytes=56 * 1024 * 1024
        ),
    )(idx, img, states, patches, w_query, w_key, w_value, w_out, w_in, w_down, w_match.reshape(1, D))


def solution(mesh):
    placed = (
        P("query", "owner", None, None, None),
        P(("query", "owner"), None, None),
        P(("query", "owner"), None),
        P(("query", "owner")),
        P(None, "tensor"),
        P(None, "tensor"),
        P(None, "tensor"),
        P("tensor", None),
        P(None, "tensor"),
        P("tensor", None),
        P(),
    )
    return jax.shard_map(
        body, mesh=mesh, in_specs=placed, out_specs=P(None, "owner"), check_vma=False
    )
```

```python
import functools

import jax
import jax.numpy as jnp
from jax import lax
from jax.experimental import pallas as pl
from jax.experimental.pallas import tpu as pltpu
from jax.sharding import PartitionSpec as P

D = 768
PATCH = 257
VIS = 1408
PAIRS = 32
NQ = 32
IMAGES = 8
SLOTS = 2
NX, NZ = 4, 8
GROUPS = NX * NZ
TENSOR = 4
PACK = 48
KEYS = 384
ROWS = PAIRS // TENSOR * NQ
EPSILON = 1e-06
MESH = pl.DeviceIdType.MESH
bf16, f32 = jnp.bfloat16, jnp.float32


def kernel(
    source, image, match_ref, states_h, patches_h, wq_h, wk_h, wv_h, wout_h, win_h, wdn_h,
    out_ref,
    states, patches, wqx, wkvx, both, img, idx_v, idx,
    qpk, qsend, qrecv, csend, crecv, keys, values, img_recv, img_s,
    ysend, yrecv, wout, win, wdn, fsend, frecv, ssend, srecv, osend, orecv,
    load_sem, img_ss, img_rs, q_ss, q_rs, c_ss, c_rs, y_ss, y_rs,
    w_own, w_ss, w_rs, f_ss, f_rs, s_ss, s_rs, o_ss, o_rs, img_sem, idx_sem,
):
    me = lax.axis_index("query")
    core = lax.axis_index("owner")
    ty = lax.axis_index("tensor")
    x, z = me // NZ, me % NZ

    def peer(k):
        iz, ix = k // NX, k % NX
        dz = ((iz + 1) // 2) * (2 * (iz % 2) - 1)
        dx = ((ix + 1) // 2) * (2 * (ix % 2) - 1)
        return ((x + dx + NX) % NX) * NZ + (z + dz + NZ) % NZ

    def y_peer(k):
        return (ty + k) % TENSOR

    def remote(src, dst, ss, rs, **device):
        return pltpu.make_async_remote_copy(
            src_ref=src, dst_ref=dst, send_sem=ss, recv_sem=rs, device_id=device, device_id_type=MESH
        )

    loads = [
        pltpu.make_async_copy(src, dst, load_sem.at[i])
        for i, (src, dst) in enumerate(
            (
                (states_h, states),
                (wq_h, wqx.at[pl.ds(0, 192)]),
                (wk_h, wkvx.at[pl.ds(0, 192)]),
                (wv_h, wkvx.at[pl.ds(256, 192)]),
                (patches_h, patches),
            )
        )
    ]
    for copy in loads:
        copy.start()

    barrier = pltpu.get_barrier_semaphore()

    @pl.loop(1, GROUPS)
    def _(k):
        pl.semaphore_signal(barrier, inc=1, device_id={"query": peer(k)}, device_id_type=MESH)

    for k in range(1, TENSOR):
        pl.semaphore_signal(barrier, inc=1, device_id={"tensor": y_peer(k)}, device_id_type=MESH)
    pl.semaphore_signal(barrier, inc=1, device_id={"owner": 1 - core}, device_id_type=MESH)

    wide = (PAIRS, 128)
    lanes = lax.broadcasted_iota(jnp.int32, wide, 1)
    number = lax.broadcasted_iota(jnp.int32, wide, 0)

    def row_of(v):
        return jnp.sum(v, axis=0, keepdims=True)

    def column_of(v):
        return jnp.sum(jnp.where(lanes == number, v, 0), axis=1, keepdims=True)

    source_row = jnp.concatenate([source[...], jnp.full((1, 128 - PAIRS), -1, jnp.int32)], axis=1)
    image_row = jnp.concatenate([image[...], jnp.zeros((1, 128 - PAIRS), jnp.int32)], axis=1)
    earlier = (column_of(source_row) == source_row) & (number < lanes)
    slot_row = source_row * SLOTS + row_of(earlier.astype(jnp.int32))
    placed = column_of(slot_row) == lanes
    img[...] = row_of(jnp.where(placed, column_of(image_row), 0))
    idx_v[0:1] = row_of(jnp.where(placed, number, 0))
    idx_v[1:2] = slot_row
    to_index = pltpu.make_async_copy(idx_v, idx, idx_sem)
    to_index.start()

    loads[0].wait()
    loads[1].wait()
    wqx[192:256] = wqx[128:192]
    low = lax.broadcasted_iota(jnp.int32, (1, 128), 1) < 64

    def times(a, b):
        return lax.dot_general(a, b, (((1,), (1,)), ((), ())), preferred_element_type=f32)

    @pl.loop(0, PAIRS // 4)
    def _(b):
        rows = states[pl.ds(b * 4, 4)].reshape(4 * NQ, D)
        q = times(rows, wqx[...]).reshape(4, NQ, 256)
        first, second = q[:, :, :128], q[:, :, 128:]
        last = jnp.where(low[None], second[:, :16], second[:, 16:])
        qpk[pl.ds(b * 4, 4)] = jnp.concatenate([first, last], axis=1).astype(bf16)

    pl.semaphore_wait(barrier, GROUPS + TENSOR - 1)
    to_index.wait()

    def img_copy(dst, src):
        return remote(img, img_recv.at[src], img_ss.at[dst], img_rs.at[src], query=dst)

    @pl.loop(1, GROUPS)
    def _(k):
        img_copy(peer(k), me).start()

    def of(ref, p):
        return ref.at[pl.ds(p * SLOTS, SLOTS)]

    def q_copy(dst, src):
        return remote(of(qsend, dst), of(qrecv, src), q_ss.at[dst], q_rs.at[src], query=dst)

    def c_copy(dst, src):
        return remote(of(csend, dst), of(crecv, src), c_ss.at[dst], c_rs.at[src], query=dst)

    @pl.loop(0, GROUPS)
    def _(k):
        p = peer(k)
        for s in range(SLOTS):
            qsend[p * SLOTS + s] = qpk[idx[0, p * SLOTS + s]]

        @pl.when(k > 0)
        def _():
            q_copy(p, me).start()

    right, left, across = y_peer(1), y_peer(3), y_peer(2)
    shards = ((wout_h, wout, 192), (win_h, win, D), (wdn_h, wdn, D))

    def part(ref, t, size, begin, length):
        return ref.at[t, pl.ds(begin, length)]

    def own(i):
        src, dst, size = shards[i]
        return pltpu.make_async_copy(src, dst.at[ty, pl.ds(0, size)], w_own.at[i])

    def first_hop(i, to_right):
        src, dst, size = shards[i]
        begin = pl.multiple_of(core * (size // 2), size // 2)
        j = 0 if to_right else 1
        return remote(
            src.at[pl.ds(begin, size // 2)], dst.at[ty, pl.ds(begin, size // 2)],
            w_ss.at[i, j], w_rs.at[i, j], tensor=right if to_right else left,
        )

    def second_hop(i, to_right, receive=False):
        _, dst, size = shards[i]
        quarter = size // 4
        t = across if receive else (left if to_right else right)
        begin = pl.multiple_of(core * (size // 2) + (0 if to_right else quarter), quarter)
        place = dst.at[t, pl.ds(begin, quarter)]
        j = 2 if to_right else 3
        return remote(place, place, w_ss.at[i, j], w_rs.at[i, j], tensor=right if to_right else left)

    def sibling(i, which, receive=False):
        _, dst, size = shards[i]
        c = 1 - core if receive else core
        quarter = size // 4
        if which < 2:
            t, begin, length = (left if which == 0 else right), c * (size // 2), size // 2
        else:
            t, begin, length = across, c * (size // 2) + (which - 2) * quarter, quarter
        place = dst.at[t, pl.ds(pl.multiple_of(begin, quarter), length)]
        return remote(place, place, w_ss.at[i, 4 + which], w_rs.at[i, 4 + which], owner=1 - core)

    def weights_0(i):
        own(i).start()
        first_hop(i, True).start()
        first_hop(i, False).start()

    def weights_1(i):
        first_hop(i, True).wait_recv()
        second_hop(i, True).start()
        sibling(i, 0).start()
        first_hop(i, False).wait_recv()
        second_hop(i, False).start()
        sibling(i, 1).start()

    def weights_2(i):
        second_hop(i, True, True).wait_recv()
        sibling(i, 2).start()
        second_hop(i, False, True).wait_recv()
        sibling(i, 3).start()

    def weights_3(i):
        for which in range(4):
            sibling(i, which, True).wait_recv()
        own(i).wait()

    for i in range(3):
        weights_0(i)

    for copy in loads[2:]:
        copy.wait()
    wkvx[192:256] = wkvx[128:192]
    wkvx[448:512] = wkvx[384:448]

    @pl.loop(0, 8)
    def _(i):
        rows = patches[pl.ds(i * 32, 32)].reshape(256, VIS)
        result = times(rows, wkvx[...])
        for c in range(4):
            both[c, pl.ds(i * 256, 256)] = result[:, c * 128 : c * 128 + 128]

    result = times(patches[256], wkvx[...])
    for c in range(4):
        both[c, 2048:2056] = result[:, c * 128 : c * 128 + 128]

    @pl.loop(0, IMAGES)
    def _(i):
        pad = jnp.zeros((KEYS - 256, 256), bf16)
        keys[i, 256:KEYS] = pad
        values[i, 256:KEYS] = pad
        for c in range(4):
            ref = keys if c < 2 else values
            part = both[c, pl.ds(i, PATCH, stride=IMAGES)].astype(bf16)
            ref[i, 0:PATCH, (c % 2) * 128 : (c % 2) * 128 + 128] = part

    img_recv[me] = img[...]

    @pl.loop(1, GROUPS)
    def _(k):
        p = peer(k)
        img_copy(p, p).wait_recv()

    to_scalars = pltpu.make_async_copy(img_recv, img_s, img_sem)
    to_scalars.start()
    to_scalars.wait()

    first_mask = low.astype(f32).astype(bf16)
    second_mask = (1 - low.astype(f32)).astype(bf16)
    column = lax.broadcasted_iota(jnp.int32, (1, KEYS), 1)

    def attend(rows, image):
        a, b = rows[0:32], rows[32:48]
        top = jnp.concatenate([a * first_mask, a * second_mask, jnp.zeros((32, 128), bf16)], axis=0)
        bottom = jnp.concatenate([jnp.zeros((64, 128), bf16), b * first_mask, b * second_mask], axis=0)
        q = jnp.concatenate([top, bottom], axis=1)
        scores = times(q, keys[image])
        scores = jnp.where(column < PATCH, scores * 0.125, -jnp.inf)
        raised = jnp.exp(scores - jnp.max(scores, axis=1, keepdims=True))
        weights = (raised / jnp.sum(raised, axis=1, keepdims=True)).astype(bf16)
        c = jnp.dot(weights, values[image], preferred_element_type=f32)
        c01 = jnp.where(low, c[0:32, :128], c[32:64, :128])
        c2 = jnp.where(low, c[64:80, 128:], c[80:96, 128:])
        return jnp.concatenate([c01, c2], axis=0).astype(bf16)

    qrecv[pl.ds(me * SLOTS, SLOTS)] = qsend[pl.ds(me * SLOTS, SLOTS)]

    @pl.loop(0, GROUPS)
    def _(k):
        p = peer(k)

        @pl.when(k > 0)
        def _():
            q_copy(p, p).wait_recv()

        done = [attend(qrecv[p * SLOTS + s], img_s[p, 0, me * SLOTS + s]) for s in range(SLOTS)]
        for s in range(SLOTS):
            csend[p * SLOTS + s] = done[s]

        @pl.when(k > 0)
        def _():
            c_copy(p, me).start()

    for i in range(3):
        weights_1(i)

    crecv[pl.ds(me * SLOTS, SLOTS)] = csend[pl.ds(me * SLOTS, SLOTS)]

    @pl.loop(1, GROUPS)
    def _(k):
        p = peer(k)
        c_copy(p, p).wait_recv()

    @pl.loop(0, PAIRS)
    def _(j):
        ysend[j // 8, j % 8] = crecv[idx[1, j]]

    def y_copy(dst, src):
        return remote(ysend.at[dst], yrecv.at[src], y_ss.at[dst], y_rs.at[src], tensor=dst)

    for k in range(1, TENSOR):
        y_copy(y_peer(k), ty).start()
    yrecv[ty] = ysend[ty]

    for i in range(3):
        weights_2(i)
    weights_3(0)
    for t in range(TENSOR):
        wout[t, 192:256] = wout[t, 128:192]
    for k in range(1, TENSOR):
        t = y_peer(k)
        y_copy(t, t).wait_recv()

    def norm(v):
        mean = jnp.mean(v, axis=-1, keepdims=True)
        squares = jnp.mean(v * v, axis=-1, keepdims=True)
        return (v - mean) * lax.rsqrt(squares - mean * mean + EPSILON)

    total = states[pl.ds(ty * 8, 8)].reshape(ROWS, D).astype(f32)
    for t in range(TENSOR):
        c = yrecv[t]
        b = c[:, 32:]
        second = jnp.concatenate([b * first_mask[None], b * second_mask[None]], axis=1)
        rows = jnp.concatenate([c[:, :32], second], axis=2).reshape(ROWS, 256)
        total = total + jnp.dot(rows, wout[t], preferred_element_type=f32)
    first_norm = norm(total).astype(bf16)

    for i in (1, 2):
        weights_3(i)
    total = first_norm.astype(f32)
    for t in range(TENSOR):
        for n in range(0, D, 256):
            up = jnp.dot(first_norm, win[t, :, n : n + 256], preferred_element_type=f32)
            hidden = (0.5 * up * (1.0 + lax.erf(up * 0.7071067811865476))).astype(bf16)
            total = total + jnp.dot(hidden, wdn[t, n : n + 256, :], preferred_element_type=f32)
    score = jnp.sum(norm(total) * match_ref[...].astype(f32).reshape(1, D), axis=-1, keepdims=True)
    score = jnp.mean(score.reshape(8, NQ, 1), axis=1)

    lane = lax.broadcasted_iota(jnp.int32, (8, 128), 1)
    pair = lax.broadcasted_iota(jnp.int32, (8, 128), 0) + (core * PAIRS + ty * 8)
    row = jnp.sum(jnp.where(lane == pair, score, 0.0), axis=0, keepdims=True)
    fsend[...] = row

    def f_copy(dst, src):
        return remote(fsend, frecv.at[src], f_ss.at[dst], f_rs.at[src], tensor=dst)

    for k in range(1, TENSOR):
        f_copy(y_peer(k), ty).start()
    frecv[ty] = row
    for k in range(1, TENSOR):
        t = y_peer(k)
        f_copy(t, t).wait_recv()
    row = frecv[0] + frecv[1] + frecv[2] + frecv[3]
    ssend[...] = row
    s_copy = remote(ssend, srecv, s_ss, s_rs, owner=1 - core)
    s_copy.start()
    s_copy.wait_recv()
    row = row + srecv[...]
    valid = lax.broadcasted_iota(jnp.int32, (1, 128), 1) < 2 * PAIRS
    partition = jnp.sum(jnp.where(valid, jnp.exp(row), 0.0), axis=1, keepdims=True)
    row = row - jnp.log(partition)
    row = jnp.where(core == 0, row, pltpu.roll(row, 128 - PAIRS, 1))
    osend[...] = row
    orecv[me] = row

    def o_copy(dst, src):
        return remote(osend, orecv.at[src], o_ss.at[dst], o_rs.at[src], query=dst)

    @pl.loop(1, GROUPS)
    def _(k):
        o_copy(peer(k), me).start()

    @pl.loop(1, GROUPS)
    def _(k):
        p = peer(k)
        o_copy(p, p).wait_recv()

    out_ref[...] = orecv[...].reshape(GROUPS, 128)[:, :PAIRS]

    @pl.loop(1, GROUPS)
    def _(k):
        p = peer(k)
        img_copy(p, p).wait_send()
        q_copy(p, p).wait_send()
        c_copy(p, p).wait_send()
        o_copy(p, p).wait_send()

    for k in range(1, TENSOR):
        t = y_peer(k)
        y_copy(t, t).wait_send()
        f_copy(t, t).wait_send()
    s_copy.wait_send()
    for i in range(3):
        first_hop(i, True).wait_send()
        first_hop(i, False).wait_send()
        second_hop(i, True).wait_send()
        second_hop(i, False).wait_send()
        for which in range(4):
            sibling(i, which).wait_send()


def body(
    patches, states, pair_source, pair_image, w_query, w_key, w_value, w_out, w_in, w_down, w_match
):
    vmem = pl.BlockSpec(memory_space=pltpu.VMEM)
    hbm = pl.BlockSpec(memory_space=pl.ANY)
    dma = pltpu.SemaphoreType.DMA
    return pl.pallas_call(
        kernel,
        out_shape=jax.ShapeDtypeStruct((GROUPS, PAIRS), f32),
        in_specs=[vmem] * 3 + [hbm] * 8,
        out_specs=vmem,
        scratch_shapes=[
            pltpu.VMEM((PAIRS, NQ, D), bf16),
            pltpu.VMEM((PATCH, IMAGES, VIS), bf16),
            pltpu.VMEM((256, D), bf16),
            pltpu.VMEM((512, VIS), bf16),
            pltpu.VMEM((4, PATCH * IMAGES, 128), f32),
            pltpu.VMEM((1, 128), jnp.int32),
            pltpu.VMEM((2, 128), jnp.int32),
            pltpu.SMEM((2, 128), jnp.int32),
            pltpu.VMEM((PAIRS, PACK, 128), bf16),
            pltpu.VMEM((GROUPS * SLOTS, PACK, 128), bf16),
            pltpu.VMEM((GROUPS * SLOTS, PACK, 128), bf16),
            pltpu.VMEM((GROUPS * SLOTS, PACK, 128), bf16),
            pltpu.VMEM((GROUPS * SLOTS, PACK, 128), bf16),
            pltpu.VMEM((IMAGES, KEYS, 256), bf16),
            pltpu.VMEM((IMAGES, KEYS, 256), bf16),
            pltpu.VMEM((GROUPS, 1, 128), jnp.int32),
            pltpu.SMEM((GROUPS, 1, 128), jnp.int32),
            pltpu.VMEM((TENSOR, 8, PACK, 128), bf16),
            pltpu.VMEM((TENSOR, 8, PACK, 128), bf16),
            pltpu.VMEM((TENSOR, 256, D), bf16),
            pltpu.VMEM((TENSOR, D, D), bf16),
            pltpu.VMEM((TENSOR, D, D), bf16),
            pltpu.VMEM((1, 128), f32),
            pltpu.VMEM((TENSOR, 1, 128), f32),
            pltpu.VMEM((1, 128), f32),
            pltpu.VMEM((1, 128), f32),
            pltpu.VMEM((1, 128), f32),
            pltpu.VMEM((GROUPS, 1, 128), f32),
            dma((5,)),
            dma((GROUPS,)), dma((GROUPS,)),
            dma((GROUPS,)), dma((GROUPS,)),
            dma((GROUPS,)), dma((GROUPS,)),
            dma((TENSOR,)), dma((TENSOR,)),
            dma((3,)), dma((3, 8)), dma((3, 8)),
            dma((TENSOR,)), dma((TENSOR,)),
            dma, dma,
            dma((GROUPS,)), dma((GROUPS,)),
            dma, dma,
        ],
        compiler_params=pltpu.CompilerParams(
            collective_id=0, has_side_effects=True, vmem_limit_bytes=56 * 1024 * 1024
        ),
    )(
        pair_source.reshape(1, PAIRS), pair_image.reshape(1, PAIRS), w_match, states,
        jnp.transpose(patches[0, 0], (1, 0, 2)), w_query.T, w_key.T, w_value.T, w_out, w_in, w_down,
    )


def solution(mesh):
    placed = (
        P("query", "owner", None, None, None),
        P(("query", "owner"), None, None),
        P(("query", "owner"), None),
        P(("query", "owner")),
        P(None, "tensor"),
        P(None, "tensor"),
        P(None, "tensor"),
        P("tensor", None),
        P(None, "tensor"),
        P("tensor", None),
        P(),
    )
    return jax.shard_map(
        body, mesh=mesh, in_specs=placed, out_specs=P(None, "owner"), check_vma=False
    )
```

```python
import functools

import jax
import jax.numpy as jnp
from jax import lax
from jax.experimental import pallas as pl
from jax.experimental.pallas import tpu as pltpu
from jax.sharding import PartitionSpec as P

D = 768
PATCH = 257
VIS = 1408
PAIRS = 32
NQ = 32
IMAGES = 8
SLOTS = 2
NX, NZ = 4, 8
GROUPS = NX * NZ
TENSOR = 4
PACK = 48
KEYS = 384
ROWS = PAIRS // TENSOR * NQ
EPSILON = 1e-06
MESH = pl.DeviceIdType.MESH
bf16, f32 = jnp.bfloat16, jnp.float32


def kernel(
    source, image, match_ref, states_h, patches_h, wq_h, wk_h, wv_h, wout_h, win_h, wdn_h,
    out_ref,
    states, patches, wqx, wkvx, both, img, idx_v, idx,
    qpk, qsend, qrecv, csend, crecv, keys, values, img_recv, img_s,
    ysend, yrecv, wout, win, wdn, fsend, frecv, ssend, srecv, osend, orecv,
    load_sem, img_ss, img_rs, q_ss, q_rs, c_ss, c_rs, y_ss, y_rs,
    w_own, w_ss, w_rs, f_ss, f_rs, s_ss, s_rs, o_ss, o_rs, img_sem, idx_sem,
):
    me = lax.axis_index("query")
    core = lax.axis_index("owner")
    ty = lax.axis_index("tensor")
    x, z = lax.div(me, NZ), lax.rem(me, NZ)

    def step(i):
        return lax.div(i + 1, 2) * (2 * lax.rem(i, 2) - 1)

    def peer(k):
        return lax.rem(x + step(lax.rem(k, NX)) + NX, NX) * NZ + lax.rem(z + step(lax.div(k, NX)) + NZ, NZ)

    steps = [((i + 1) // 2) * (2 * (i % 2) - 1) for i in range(NZ)]
    columns = [lax.rem(x + steps[i] + NX, NX) * NZ for i in range(NX)]
    rows_z = [lax.rem(z + steps[i] + NZ, NZ) for i in range(NZ)]
    peers = [columns[k % NX] + rows_z[k // NX] for k in range(GROUPS)]
    others = peers[1:]

    def y_peer(k):
        return lax.rem(ty + k, TENSOR)

    def remote(src, dst, ss, rs, **device):
        return pltpu.make_async_remote_copy(
            src_ref=src, dst_ref=dst, send_sem=ss, recv_sem=rs, device_id=device, device_id_type=MESH
        )

    loads = [
        pltpu.make_async_copy(src, dst, load_sem.at[i])
        for i, (src, dst) in enumerate(
            (
                (states_h, states),
                (wq_h, wqx.at[pl.ds(0, 192)]),
                (wk_h, wkvx.at[pl.ds(0, 192)]),
                (wv_h, wkvx.at[pl.ds(256, 192)]),
                (patches_h, patches),
            )
        )
    ]
    for copy in loads:
        copy.start()

    barrier = pltpu.get_barrier_semaphore()

    for p in reversed(others):
        pl.semaphore_signal(barrier, inc=1, device_id={"query": p}, device_id_type=MESH)

    for k in range(1, TENSOR):
        pl.semaphore_signal(barrier, inc=1, device_id={"tensor": y_peer(k)}, device_id_type=MESH)
    pl.semaphore_signal(barrier, inc=1, device_id={"owner": 1 - core}, device_id_type=MESH)

    wide = (PAIRS, 128)
    lanes = lax.broadcasted_iota(jnp.int32, wide, 1)
    number = lax.broadcasted_iota(jnp.int32, wide, 0)

    def row_of(v):
        return jnp.sum(v, axis=0, keepdims=True)

    def column_of(v):
        return jnp.sum(jnp.where(lanes == number, v, 0), axis=1, keepdims=True)

    source_row = jnp.concatenate([source[...], jnp.full((1, 128 - PAIRS), -1, jnp.int32)], axis=1)
    image_row = jnp.concatenate([image[...], jnp.zeros((1, 128 - PAIRS), jnp.int32)], axis=1)
    earlier = (column_of(source_row) == source_row) & (number < lanes)
    slot_row = source_row * SLOTS + row_of(earlier.astype(jnp.int32))
    placed = column_of(slot_row) == lanes
    img[...] = row_of(jnp.where(placed, column_of(image_row), 0))
    idx_v[0:1] = row_of(jnp.where(placed, number, 0))
    idx_v[1:2] = slot_row
    to_index = pltpu.make_async_copy(idx_v, idx, idx_sem)
    to_index.start()

    loads[0].wait()
    loads[1].wait()
    wqx[192:256] = wqx[128:192]
    low = lax.broadcasted_iota(jnp.int32, (1, 128), 1) < 64

    def times(a, b):
        return lax.dot_general(a, b, (((1,), (1,)), ((), ())), preferred_element_type=f32)

    q = times(states[...].reshape(PAIRS * NQ, D), wqx[...]).reshape(PAIRS, NQ, 256)
    last = jnp.where(low[None], q[:, :16, 128:], q[:, 16:, 128:])
    qpk[...] = jnp.concatenate([q[:, :, :128], last], axis=1).astype(bf16)

    pl.semaphore_wait(barrier, GROUPS + TENSOR - 1)
    to_index.wait()

    def img_copy(dst, src):
        return remote(img, img_recv.at[src], img_ss.at[dst], img_rs.at[src], query=dst)

    for p in others:
        img_copy(p, me).start()

    def of(ref, p):
        return ref.at[pl.ds(p * SLOTS, SLOTS)]

    def q_copy(dst, src):
        return remote(of(qsend, dst), of(qrecv, src), q_ss.at[dst], q_rs.at[src], query=dst)

    def c_copy(dst, src):
        return remote(of(csend, dst), of(crecv, src), c_ss.at[dst], c_rs.at[src], query=dst)

    for k, p in enumerate(peers):
        for s in range(SLOTS):
            qsend[p * SLOTS + s] = qpk[idx[0, p * SLOTS + s]]
        if k:
            q_copy(p, me).start()

    right, left, across = y_peer(1), y_peer(3), y_peer(2)
    shards = ((wout_h, wout, 192), (win_h, win, D), (wdn_h, wdn, D))

    def part(ref, t, size, begin, length):
        return ref.at[t, pl.ds(begin, length)]

    def own(i):
        src, dst, size = shards[i]
        return pltpu.make_async_copy(src, dst.at[ty, pl.ds(0, size)], w_own.at[i])

    def first_hop(i, to_right):
        src, dst, size = shards[i]
        begin = pl.multiple_of(core * (size // 2), size // 2)
        j = 0 if to_right else 1
        return remote(
            src.at[pl.ds(begin, size // 2)], dst.at[ty, pl.ds(begin, size // 2)],
            w_ss.at[i, j], w_rs.at[i, j], tensor=right if to_right else left,
        )

    def second_hop(i, to_right, receive=False):
        _, dst, size = shards[i]
        quarter = size // 4
        t = across if receive else (left if to_right else right)
        begin = pl.multiple_of(core * (size // 2) + (0 if to_right else quarter), quarter)
        place = dst.at[t, pl.ds(begin, quarter)]
        j = 2 if to_right else 3
        return remote(place, place, w_ss.at[i, j], w_rs.at[i, j], tensor=right if to_right else left)

    def sibling(i, which, receive=False):
        _, dst, size = shards[i]
        c = 1 - core if receive else core
        quarter = size // 4
        if which < 2:
            t, begin, length = (left if which == 0 else right), c * (size // 2), size // 2
        else:
            t, begin, length = across, c * (size // 2) + (which - 2) * quarter, quarter
        place = dst.at[t, pl.ds(pl.multiple_of(begin, quarter), length)]
        return remote(place, place, w_ss.at[i, 4 + which], w_rs.at[i, 4 + which], owner=1 - core)

    def weights_0(i):
        own(i).start()
        first_hop(i, True).start()
        first_hop(i, False).start()

    def weights_1(i):
        first_hop(i, True).wait_recv()
        second_hop(i, True).start()
        sibling(i, 0).start()
        first_hop(i, False).wait_recv()
        second_hop(i, False).start()
        sibling(i, 1).start()

    def weights_2(i):
        second_hop(i, True, True).wait_recv()
        sibling(i, 2).start()
        second_hop(i, False, True).wait_recv()
        sibling(i, 3).start()

    def weights_3(i):
        for which in range(4):
            sibling(i, which, True).wait_recv()
        own(i).wait()

    for i in range(3):
        weights_0(i)

    for copy in loads[2:]:
        copy.wait()
    wkvx[192:256] = wkvx[128:192]
    wkvx[448:512] = wkvx[384:448]

    @pl.loop(0, 4)
    def _(i):
        rows = patches[pl.ds(i * 64, 64)].reshape(512, VIS)
        result = times(rows, wkvx[...])
        for c in range(4):
            both[c, pl.ds(i * 512, 512)] = result[:, c * 128 : c * 128 + 128]

    result = times(patches[256], wkvx[...])
    for c in range(4):
        both[c, 2048:2056] = result[:, c * 128 : c * 128 + 128]

    @pl.loop(0, IMAGES)
    def _(i):
        pad = jnp.zeros((KEYS - 256, 256), bf16)
        keys[i, 256:KEYS] = pad
        values[i, 256:KEYS] = pad
        for c in range(4):
            ref = keys if c < 2 else values
            part = both[c, pl.ds(i, PATCH, stride=IMAGES)].astype(bf16)
            ref[i, 0:PATCH, (c % 2) * 128 : (c % 2) * 128 + 128] = part

    img_recv[me] = img[...]

    for p in others:
        img_copy(p, p).wait_recv()

    to_scalars = pltpu.make_async_copy(img_recv, img_s, img_sem)
    to_scalars.start()
    to_scalars.wait()

    first_mask = low.astype(f32).astype(bf16)
    second_mask = (1 - low.astype(f32)).astype(bf16)
    column = lax.broadcasted_iota(jnp.int32, (1, KEYS), 1)

    factor = 0.125 * 1.4426950408889634

    def attend(slots, images):
        scores, weights, context, packed = [], [], [], []
        for slot, image in zip(slots, images):
            rows = qrecv[slot]
            a, b = rows[0:32], rows[32:48]
            top = jnp.concatenate([a * first_mask, a * second_mask, jnp.zeros((32, 128), bf16)], axis=0)
            bottom = jnp.concatenate([jnp.zeros((64, 128), bf16), b * first_mask, b * second_mask], axis=0)
            scores.append(times(jnp.concatenate([top, bottom], axis=1), keys[image]))
        for s in scores:
            s = jnp.where(column < PATCH, s, -jnp.inf)
            e = jnp.exp2((s - jnp.max(s, axis=1, keepdims=True)) * factor)
            weights.append((e * (1.0 / jnp.sum(e, axis=1, keepdims=True))).astype(bf16))
        for w, image in zip(weights, images):
            context.append(jnp.dot(w, values[image], preferred_element_type=f32))
        for c in context:
            c01 = jnp.where(low, c[0:32, :128], c[32:64, :128])
            c2 = jnp.where(low, c[64:80, 128:], c[80:96, 128:])
            packed.append(jnp.concatenate([c01, c2], axis=0).astype(bf16))
        return packed

    qrecv[pl.ds(me * SLOTS, SLOTS)] = qsend[pl.ds(me * SLOTS, SLOTS)]

    @pl.loop(0, GROUPS // NX)
    def _(n):
        four = [peer(n * NX + i) for i in range(NX)]
        for i, p in enumerate(four):
            if i:
                q_copy(p, p).wait_recv()
            else:
                pl.when(n > 0)(q_copy(p, p).wait_recv)
        slots = [p * SLOTS + s for p in four for s in range(SLOTS)]
        images = [img_s[p, 0, me * SLOTS + s] for p in four for s in range(SLOTS)]
        for slot, rows in zip(slots, attend(slots, images)):
            csend[slot] = rows
        for i, p in enumerate(four):
            if i:
                c_copy(p, me).start()
            else:
                pl.when(n > 0)(c_copy(p, me).start)

    for i in range(3):
        weights_1(i)

    crecv[pl.ds(me * SLOTS, SLOTS)] = csend[pl.ds(me * SLOTS, SLOTS)]

    for p in others:
        img_copy(p, p).wait_send()
        q_copy(p, p).wait_send()
        c_copy(p, p).wait_recv()

    @pl.loop(0, PAIRS)
    def _(j):
        ysend[j // 8, j % 8] = crecv[idx[1, j]]

    def y_copy(dst, src):
        return remote(ysend.at[dst], yrecv.at[src], y_ss.at[dst], y_rs.at[src], tensor=dst)

    for k in range(1, TENSOR):
        y_copy(y_peer(k), ty).start()
    yrecv[ty] = ysend[ty]

    for p in others:
        c_copy(p, p).wait_send()

    for i in range(3):
        weights_2(i)
    weights_3(0)
    for t in range(TENSOR):
        wout[t, 192:256] = wout[t, 128:192]
    for k in range(1, TENSOR):
        t = y_peer(k)
        y_copy(t, t).wait_recv()

    def norm(v):
        mean = jnp.mean(v, axis=-1, keepdims=True)
        squares = jnp.mean(v * v, axis=-1, keepdims=True)
        return (v - mean) * lax.rsqrt(squares - mean * mean + EPSILON)

    total = states[pl.ds(ty * 8, 8)].reshape(ROWS, D).astype(f32)
    for t in range(TENSOR):
        c = yrecv[t]
        b = c[:, 32:]
        second = jnp.concatenate([b * first_mask[None], b * second_mask[None]], axis=1)
        rows = jnp.concatenate([c[:, :32], second], axis=2).reshape(ROWS, 256)
        total = total + jnp.dot(rows, wout[t], preferred_element_type=f32)
    first_norm = norm(total).astype(bf16)

    weights_3(1)
    weights_3(2)
    total = first_norm.astype(f32)

    def up(t):
        return jnp.dot(first_norm, win[t], preferred_element_type=f32)

    later = up(0)
    for t in range(TENSOR):
        now = later
        if t < TENSOR - 1:
            later = up(t + 1)
        hidden = (0.5 * now * (1.0 + lax.erf(now * 0.7071067811865476))).astype(bf16)
        total = total + jnp.dot(hidden, wdn[t], preferred_element_type=f32)
    score = jnp.sum(norm(total) * match_ref[...].astype(f32).reshape(1, D), axis=-1, keepdims=True)
    score = jnp.mean(score.reshape(8, NQ, 1), axis=1)

    lane = lax.broadcasted_iota(jnp.int32, (8, 128), 1)
    pair = lax.broadcasted_iota(jnp.int32, (8, 128), 0) + (core * PAIRS + ty * 8)
    row = jnp.sum(jnp.where(lane == pair, score, 0.0), axis=0, keepdims=True)
    fsend[...] = row

    def f_copy(dst, src):
        return remote(fsend, frecv.at[src], f_ss.at[dst], f_rs.at[src], tensor=dst)

    for k in range(1, TENSOR):
        f_copy(y_peer(k), ty).start()
    frecv[ty] = row
    for k in range(1, TENSOR):
        t = y_peer(k)
        f_copy(t, t).wait_recv()
    row = frecv[0] + frecv[1] + frecv[2] + frecv[3]
    ssend[...] = row
    s_copy = remote(ssend, srecv, s_ss, s_rs, owner=1 - core)
    s_copy.start()
    s_copy.wait_recv()
    row = row + srecv[...]
    valid = lax.broadcasted_iota(jnp.int32, (1, 128), 1) < 2 * PAIRS
    partition = jnp.sum(jnp.where(valid, jnp.exp(row), 0.0), axis=1, keepdims=True)
    row = row - jnp.log(partition)
    row = jnp.where(core == 0, row, pltpu.roll(row, 128 - PAIRS, 1))
    osend[...] = row
    orecv[me] = row

    def o_copy(dst, src):
        return remote(osend, orecv.at[src], o_ss.at[dst], o_rs.at[src], query=dst)

    for p in reversed(others):
        o_copy(p, me).start()

    for p in others:
        o_copy(p, p).wait_recv()

    out_ref[...] = orecv[...].reshape(GROUPS, 128)[:, :PAIRS]

    for p in others:
        o_copy(p, p).wait_send()

    for k in range(1, TENSOR):
        t = y_peer(k)
        y_copy(t, t).wait_send()
        f_copy(t, t).wait_send()
    s_copy.wait_send()
    for i in range(3):
        first_hop(i, True).wait_send()
        first_hop(i, False).wait_send()
        second_hop(i, True).wait_send()
        second_hop(i, False).wait_send()
        for which in range(4):
            sibling(i, which).wait_send()


def body(
    patches, states, pair_source, pair_image, w_query, w_key, w_value, w_out, w_in, w_down, w_match
):
    vmem = pl.BlockSpec(memory_space=pltpu.VMEM)
    hbm = pl.BlockSpec(memory_space=pl.ANY)
    dma = pltpu.SemaphoreType.DMA
    return pl.pallas_call(
        kernel,
        out_shape=jax.ShapeDtypeStruct((GROUPS, PAIRS), f32),
        in_specs=[vmem] * 3 + [hbm] * 8,
        out_specs=vmem,
        scratch_shapes=[
            pltpu.VMEM((PAIRS, NQ, D), bf16),
            pltpu.VMEM((PATCH, IMAGES, VIS), bf16),
            pltpu.VMEM((256, D), bf16),
            pltpu.VMEM((512, VIS), bf16),
            pltpu.VMEM((4, PATCH * IMAGES, 128), f32),
            pltpu.VMEM((1, 128), jnp.int32),
            pltpu.VMEM((2, 128), jnp.int32),
            pltpu.SMEM((2, 128), jnp.int32),
            pltpu.VMEM((PAIRS, PACK, 128), bf16),
            pltpu.VMEM((GROUPS * SLOTS, PACK, 128), bf16),
            pltpu.VMEM((GROUPS * SLOTS, PACK, 128), bf16),
            pltpu.VMEM((GROUPS * SLOTS, PACK, 128), bf16),
            pltpu.VMEM((GROUPS * SLOTS, PACK, 128), bf16),
            pltpu.VMEM((IMAGES, KEYS, 256), bf16),
            pltpu.VMEM((IMAGES, KEYS, 256), bf16),
            pltpu.VMEM((GROUPS, 1, 128), jnp.int32),
            pltpu.SMEM((GROUPS, 1, 128), jnp.int32),
            pltpu.VMEM((TENSOR, 8, PACK, 128), bf16),
            pltpu.VMEM((TENSOR, 8, PACK, 128), bf16),
            pltpu.VMEM((TENSOR, 256, D), bf16),
            pltpu.VMEM((TENSOR, D, D), bf16),
            pltpu.VMEM((TENSOR, D, D), bf16),
            pltpu.VMEM((1, 128), f32),
            pltpu.VMEM((TENSOR, 1, 128), f32),
            pltpu.VMEM((1, 128), f32),
            pltpu.VMEM((1, 128), f32),
            pltpu.VMEM((1, 128), f32),
            pltpu.VMEM((GROUPS, 1, 128), f32),
            dma((5,)),
            dma((GROUPS,)), dma((GROUPS,)),
            dma((GROUPS,)), dma((GROUPS,)),
            dma((GROUPS,)), dma((GROUPS,)),
            dma((TENSOR,)), dma((TENSOR,)),
            dma((3,)), dma((3, 8)), dma((3, 8)),
            dma((TENSOR,)), dma((TENSOR,)),
            dma, dma,
            dma((GROUPS,)), dma((GROUPS,)),
            dma, dma,
        ],
        compiler_params=pltpu.CompilerParams(
            collective_id=0, has_side_effects=True, vmem_limit_bytes=56 * 1024 * 1024
        ),
    )(
        pair_source.reshape(1, PAIRS), pair_image.reshape(1, PAIRS), w_match, states,
        jnp.transpose(patches[0, 0], (1, 0, 2)), w_query.T, w_key.T, w_value.T, w_out, w_in, w_down,
    )


def solution(mesh):
    placed = (
        P("query", "owner", None, None, None),
        P(("query", "owner"), None, None),
        P(("query", "owner"), None),
        P(("query", "owner")),
        P(None, "tensor"),
        P(None, "tensor"),
        P(None, "tensor"),
        P("tensor", None),
        P(None, "tensor"),
        P("tensor", None),
        P(),
    )
    return jax.shard_map(
        body, mesh=mesh, in_specs=placed, out_specs=P(None, "owner"), check_vma=False
    )
```

```python
import functools

import jax
import jax.numpy as jnp
from jax import lax
from jax.experimental import pallas as pl
from jax.experimental.pallas import tpu as pltpu
from jax.sharding import PartitionSpec as P

D = 768
PATCH = 257
VIS = 1408
PAIRS = 32
NQ = 32
IMAGES = 8
SLOTS = 2
NX, NZ = 4, 8
GROUPS = NX * NZ
TENSOR = 4
PACK = 48
KEYS = 384
ROWS = PAIRS // TENSOR * NQ
EPSILON = 1e-06
MESH = pl.DeviceIdType.MESH
bf16, f32 = jnp.bfloat16, jnp.float32


def kernel(
    source, image, match_ref, states_h, patches_h, wq_h, wk_h, wv_h, wout_h, win_h, wdn_h,
    out_ref,
    states, patches, wqx, wkvx, both, img, idx_v, idx,
    qpk, qsend, qrecv, csend, crecv, keys, values, img_recv, img_s,
    ysend, yrecv, wout, win, wdn, fsend, frecv, osend, orecv,
    load_sem, img_ss, img_rs, q_ss, q_rs, c_ss, c_rs, y_ss, y_rs,
    w_own, w_ss, w_rs, f_ss, f_rs, o_ss, o_rs, img_sem, idx_sem,
):
    me = lax.axis_index("query")
    core = lax.axis_index("owner")
    ty = lax.axis_index("tensor")
    x, z = lax.div(me, NZ), lax.rem(me, NZ)

    def step(i):
        return lax.div(i + 1, 2) * (2 * lax.rem(i, 2) - 1)

    def peer(k):
        return lax.rem(x + step(lax.rem(k, NX)) + NX, NX) * NZ + lax.rem(z + step(lax.div(k, NX)) + NZ, NZ)

    steps = [((i + 1) // 2) * (2 * (i % 2) - 1) for i in range(NZ)]
    columns = [lax.rem(x + steps[i] + NX, NX) * NZ for i in range(NX)]
    rows_z = [lax.rem(z + steps[i] + NZ, NZ) for i in range(NZ)]
    peers = [columns[k % NX] + rows_z[k // NX] for k in range(GROUPS)]
    others = peers[1:]

    def y_peer(k):
        return lax.rem(ty + k, TENSOR)

    def remote(src, dst, ss, rs, **device):
        return pltpu.make_async_remote_copy(
            src_ref=src, dst_ref=dst, send_sem=ss, recv_sem=rs, device_id=device, device_id_type=MESH
        )

    loads = [
        pltpu.make_async_copy(src, dst, load_sem.at[i])
        for i, (src, dst) in enumerate(
            (
                (states_h, states),
                (wq_h, wqx.at[pl.ds(0, 192)]),
                (wk_h, wkvx.at[pl.ds(0, 192)]),
                (wv_h, wkvx.at[pl.ds(256, 192)]),
                (patches_h, patches),
            )
        )
    ]
    for copy in loads:
        copy.start()

    barrier = pltpu.get_barrier_semaphore()

    for p in reversed(others):
        pl.semaphore_signal(barrier, inc=1, device_id={"query": p}, device_id_type=MESH)

    for k in range(1, TENSOR):
        pl.semaphore_signal(barrier, inc=1, device_id={"tensor": y_peer(k)}, device_id_type=MESH)
    for k in range(TENSOR):
        pl.semaphore_signal(barrier, inc=1, device_id={"owner": 1 - core, "tensor": y_peer(k)}, device_id_type=MESH)

    wide = (PAIRS, 128)
    lanes = lax.broadcasted_iota(jnp.int32, wide, 1)
    number = lax.broadcasted_iota(jnp.int32, wide, 0)

    def row_of(v):
        return jnp.sum(v, axis=0, keepdims=True)

    def column_of(v):
        return jnp.sum(jnp.where(lanes == number, v, 0), axis=1, keepdims=True)

    source_row = jnp.concatenate([source[...], jnp.full((1, 128 - PAIRS), -1, jnp.int32)], axis=1)
    image_row = jnp.concatenate([image[...], jnp.zeros((1, 128 - PAIRS), jnp.int32)], axis=1)
    earlier = (column_of(source_row) == source_row) & (number < lanes)
    slot_row = source_row * SLOTS + row_of(earlier.astype(jnp.int32))
    placed = column_of(slot_row) == lanes
    img[...] = row_of(jnp.where(placed, column_of(image_row), 0))
    idx_v[0:1] = row_of(jnp.where(placed, number, 0))
    idx_v[1:2] = slot_row
    to_index = pltpu.make_async_copy(idx_v, idx, idx_sem)
    to_index.start()

    loads[0].wait()
    loads[1].wait()
    wqx[192:256] = wqx[128:192]
    low = lax.broadcasted_iota(jnp.int32, (1, 128), 1) < 64

    def times(a, b):
        return lax.dot_general(a, b, (((1,), (1,)), ((), ())), preferred_element_type=f32)

    q = times(states[...].reshape(PAIRS * NQ, D), wqx[...]).reshape(PAIRS, NQ, 256)
    last = jnp.where(low[None], q[:, :16, 128:], q[:, 16:, 128:])
    qpk[...] = jnp.concatenate([q[:, :, :128], last], axis=1).astype(bf16)

    pl.semaphore_wait(barrier, GROUPS - 1 + 2 * TENSOR - 1)
    to_index.wait()

    right, left, across = y_peer(1), y_peer(3), y_peer(2)
    shards = ((wout_h, wout, 192), (win_h, win, D), (wdn_h, wdn, D))

    def part(ref, t, size, begin, length):
        return ref.at[t, pl.ds(begin, length)]

    def own(i):
        src, dst, size = shards[i]
        return pltpu.make_async_copy(src, dst.at[ty, pl.ds(0, size)], w_own.at[i])

    def first_hop(i, to_right):
        src, dst, size = shards[i]
        begin = pl.multiple_of(core * (size // 2), size // 2)
        j = 0 if to_right else 1
        return remote(
            src.at[pl.ds(begin, size // 2)], dst.at[ty, pl.ds(begin, size // 2)],
            w_ss.at[i, j], w_rs.at[i, j], tensor=right if to_right else left,
        )

    def second_hop(i, to_right, receive=False):
        _, dst, size = shards[i]
        quarter = size // 4
        t = across if receive else (left if to_right else right)
        begin = pl.multiple_of(core * (size // 2) + (0 if to_right else quarter), quarter)
        place = dst.at[t, pl.ds(begin, quarter)]
        j = 2 if to_right else 3
        return remote(place, place, w_ss.at[i, j], w_rs.at[i, j], tensor=right if to_right else left)

    def sibling(i, which, receive=False):
        _, dst, size = shards[i]
        c = 1 - core if receive else core
        quarter = size // 4
        if which < 2:
            t, begin, length = (left if which == 0 else right), c * (size // 2), size // 2
        else:
            t, begin, length = across, c * (size // 2) + (which - 2) * quarter, quarter
        place = dst.at[t, pl.ds(pl.multiple_of(begin, quarter), length)]
        return remote(place, place, w_ss.at[i, 4 + which], w_rs.at[i, 4 + which], owner=1 - core)

    def weights_0(i):
        own(i).start()
        first_hop(i, True).start()
        first_hop(i, False).start()

    def weights_1(i):
        first_hop(i, True).wait_recv()
        second_hop(i, True).start()
        sibling(i, 0).start()
        first_hop(i, False).wait_recv()
        second_hop(i, False).start()
        sibling(i, 1).start()

    def weights_2(i):
        second_hop(i, True, True).wait_recv()
        sibling(i, 2).start()
        second_hop(i, False, True).wait_recv()
        sibling(i, 3).start()

    def weights_3(i):
        for which in range(4):
            sibling(i, which, True).wait_recv()
        own(i).wait()

    for i in range(3):
        weights_0(i)

    def img_copy(dst, src):
        return remote(img, img_recv.at[src], img_ss.at[dst], img_rs.at[src], query=dst)

    for p in others:
        img_copy(p, me).start()

    def of(ref, p):
        return ref.at[pl.ds(p * SLOTS, SLOTS)]

    def q_copy(dst, src):
        return remote(of(qsend, dst), of(qrecv, src), q_ss.at[dst], q_rs.at[src], query=dst)

    def c_copy(dst, src):
        return remote(of(csend, dst), of(crecv, src), c_ss.at[dst], c_rs.at[src], query=dst)

    for k, p in enumerate(peers):
        for s in range(SLOTS):
            qsend[p * SLOTS + s] = qpk[idx[0, p * SLOTS + s]]
        if k:
            q_copy(p, me).start()

    for copy in loads[2:]:
        copy.wait()
    wkvx[192:256] = wkvx[128:192]
    wkvx[448:512] = wkvx[384:448]

    @pl.loop(0, 4)
    def _(i):
        rows = patches[pl.ds(i * 64, 64)].reshape(512, VIS)
        result = times(rows, wkvx[...])
        for c in range(4):
            both[c, pl.ds(i * 512, 512)] = result[:, c * 128 : c * 128 + 128]

    result = times(patches[256], wkvx[...])
    for c in range(4):
        both[c, 2048:2056] = result[:, c * 128 : c * 128 + 128]

    @pl.loop(0, IMAGES)
    def _(i):
        pad = jnp.zeros((KEYS - 256, 256), bf16)
        keys[i, 256:KEYS] = pad
        values[i, 256:KEYS] = pad
        for c in range(4):
            ref = keys if c < 2 else values
            part = both[c, pl.ds(i, PATCH, stride=IMAGES)].astype(bf16)
            ref[i, 0:PATCH, (c % 2) * 128 : (c % 2) * 128 + 128] = part

    img_recv[me] = img[...]

    for p in others:
        img_copy(p, p).wait_recv()

    to_scalars = pltpu.make_async_copy(img_recv, img_s, img_sem)
    to_scalars.start()
    to_scalars.wait()

    first_mask = low.astype(f32).astype(bf16)
    second_mask = (1 - low.astype(f32)).astype(bf16)
    column = lax.broadcasted_iota(jnp.int32, (1, KEYS), 1)

    factor = 0.125 * 1.4426950408889634

    def attend(slots, images):
        scores, weights, context, packed = [], [], [], []
        for slot, image in zip(slots, images):
            rows = qrecv[slot]
            a, b = rows[0:32], rows[32:48]
            top = jnp.concatenate([a * first_mask, a * second_mask, jnp.zeros((32, 128), bf16)], axis=0)
            bottom = jnp.concatenate([jnp.zeros((64, 128), bf16), b * first_mask, b * second_mask], axis=0)
            scores.append(times(jnp.concatenate([top, bottom], axis=1), keys[image]))
        for s in scores:
            s = jnp.where(column < PATCH, s, -jnp.inf)
            e = jnp.exp2((s - jnp.max(s, axis=1, keepdims=True)) * factor)
            weights.append((e * (1.0 / jnp.sum(e, axis=1, keepdims=True))).astype(bf16))
        for w, image in zip(weights, images):
            context.append(jnp.dot(w, values[image], preferred_element_type=f32))
        for c in context:
            c01 = jnp.where(low, c[0:32, :128], c[32:64, :128])
            c2 = jnp.where(low, c[64:80, 128:], c[80:96, 128:])
            packed.append(jnp.concatenate([c01, c2], axis=0).astype(bf16))
        return packed

    qrecv[pl.ds(me * SLOTS, SLOTS)] = qsend[pl.ds(me * SLOTS, SLOTS)]

    @pl.loop(0, GROUPS // NX)
    def _(n):
        four = [peer(n * NX + i) for i in range(NX)]
        for i, p in enumerate(four):
            if i:
                q_copy(p, p).wait_recv()
            else:
                pl.when(n > 0)(q_copy(p, p).wait_recv)
        @pl.when(n == GROUPS // NX - 1)
        def _():
            for i in range(3):
                weights_1(i)

        slots = [p * SLOTS + s for p in four for s in range(SLOTS)]
        images = [img_s[p, 0, me * SLOTS + s] for p in four for s in range(SLOTS)]
        for slot, rows in zip(slots, attend(slots, images)):
            csend[slot] = rows
        for i, p in enumerate(four):
            if i:
                c_copy(p, me).start()
            else:
                pl.when(n > 0)(c_copy(p, me).start)

    crecv[pl.ds(me * SLOTS, SLOTS)] = csend[pl.ds(me * SLOTS, SLOTS)]

    for p in others:
        img_copy(p, p).wait_send()
        q_copy(p, p).wait_send()
        c_copy(p, p).wait_recv()

    @pl.loop(0, PAIRS)
    def _(j):
        ysend[j // 8, j % 8] = crecv[idx[1, j]]

    def y_copy(dst, src):
        return remote(ysend.at[dst], yrecv.at[src], y_ss.at[dst], y_rs.at[src], tensor=dst)

    for k in range(1, TENSOR):
        y_copy(y_peer(k), ty).start()
    yrecv[ty] = ysend[ty]

    for p in others:
        c_copy(p, p).wait_send()

    for i in range(3):
        weights_2(i)
    weights_3(0)
    for t in range(TENSOR):
        wout[t, 192:256] = wout[t, 128:192]
    for k in range(1, TENSOR):
        t = y_peer(k)
        y_copy(t, t).wait_recv()

    def norm(v):
        mean = jnp.mean(v, axis=-1, keepdims=True)
        squares = jnp.mean(v * v, axis=-1, keepdims=True)
        return (v - mean) * lax.rsqrt(squares - mean * mean + EPSILON)

    total = states[pl.ds(ty * 8, 8)].reshape(ROWS, D).astype(f32)
    for t in range(TENSOR):
        c = yrecv[t]
        b = c[:, 32:]
        second = jnp.concatenate([b * first_mask[None], b * second_mask[None]], axis=1)
        rows = jnp.concatenate([c[:, :32], second], axis=2).reshape(ROWS, 256)
        total = total + jnp.dot(rows, wout[t], preferred_element_type=f32)
    first_norm = norm(total).astype(bf16)

    weights_3(1)
    weights_3(2)
    total = first_norm.astype(f32)

    def up(t):
        return jnp.dot(first_norm, win[t], preferred_element_type=f32)

    later = up(0)
    for t in range(TENSOR):
        now = later
        if t < TENSOR - 1:
            later = up(t + 1)
        hidden = (0.5 * now * (1.0 + lax.erf(now * 0.7071067811865476))).astype(bf16)
        total = total + jnp.dot(hidden, wdn[t], preferred_element_type=f32)
    score = jnp.sum(norm(total) * match_ref[...].astype(f32).reshape(1, D), axis=-1, keepdims=True)
    score = jnp.mean(score.reshape(8, NQ, 1), axis=1)

    lane = lax.broadcasted_iota(jnp.int32, (8, 128), 1)
    pair = lax.broadcasted_iota(jnp.int32, (8, 128), 0) + (core * PAIRS + ty * 8)
    row = jnp.sum(jnp.where(lane == pair, score, 0.0), axis=0, keepdims=True)
    fsend[...] = row
    frecv[core, ty] = row
    group = [(c, k) for c in (0, 1) for k in range(TENSOR) if c or k]

    def f_copy(c, k, receive=False):
        device = {"owner": lax.rem(core + c, 2), "tensor": y_peer(k)}
        at = (device["owner"], device["tensor"]) if receive else (core, ty)
        return remote(fsend, frecv.at[at], f_ss.at[c, k], f_rs.at[at], **device)

    for c, k in reversed(group):
        f_copy(c, k).start()
    for c, k in group:
        f_copy(c, k, True).wait_recv()
    row = jnp.sum(frecv[...].reshape(2 * TENSOR, 128), axis=0, keepdims=True)
    valid = lax.broadcasted_iota(jnp.int32, (1, 128), 1) < 2 * PAIRS
    partition = jnp.sum(jnp.where(valid, jnp.exp(row), 0.0), axis=1, keepdims=True)
    row = row - jnp.log(partition)
    row = jnp.where(core == 0, row, pltpu.roll(row, 128 - PAIRS, 1))
    osend[...] = row
    orecv[me] = row

    def o_copy(dst, src):
        return remote(osend, orecv.at[src], o_ss.at[dst], o_rs.at[src], query=dst)

    for p in reversed(others):
        o_copy(p, me).start()

    for p in others:
        o_copy(p, p).wait_recv()

    out_ref[...] = orecv[...].reshape(GROUPS, 128)[:, :PAIRS]

    for p in others:
        o_copy(p, p).wait_send()

    for k in range(1, TENSOR):
        t = y_peer(k)
        y_copy(t, t).wait_send()
    for c, k in group:
        f_copy(c, k).wait_send()
    for i in range(3):
        first_hop(i, True).wait_send()
        first_hop(i, False).wait_send()
        second_hop(i, True).wait_send()
        second_hop(i, False).wait_send()
        for which in range(4):
            sibling(i, which).wait_send()


def body(
    patches, states, pair_source, pair_image, w_query, w_key, w_value, w_out, w_in, w_down, w_match
):
    vmem = pl.BlockSpec(memory_space=pltpu.VMEM)
    hbm = pl.BlockSpec(memory_space=pl.ANY)
    dma = pltpu.SemaphoreType.DMA
    return pl.pallas_call(
        kernel,
        out_shape=jax.ShapeDtypeStruct((GROUPS, PAIRS), f32),
        in_specs=[vmem] * 3 + [hbm] * 8,
        out_specs=vmem,
        scratch_shapes=[
            pltpu.VMEM((PAIRS, NQ, D), bf16),
            pltpu.VMEM((PATCH, IMAGES, VIS), bf16),
            pltpu.VMEM((256, D), bf16),
            pltpu.VMEM((512, VIS), bf16),
            pltpu.VMEM((4, PATCH * IMAGES, 128), f32),
            pltpu.VMEM((1, 128), jnp.int32),
            pltpu.VMEM((2, 128), jnp.int32),
            pltpu.SMEM((2, 128), jnp.int32),
            pltpu.VMEM((PAIRS, PACK, 128), bf16),
            pltpu.VMEM((GROUPS * SLOTS, PACK, 128), bf16),
            pltpu.VMEM((GROUPS * SLOTS, PACK, 128), bf16),
            pltpu.VMEM((GROUPS * SLOTS, PACK, 128), bf16),
            pltpu.VMEM((GROUPS * SLOTS, PACK, 128), bf16),
            pltpu.VMEM((IMAGES, KEYS, 256), bf16),
            pltpu.VMEM((IMAGES, KEYS, 256), bf16),
            pltpu.VMEM((GROUPS, 1, 128), jnp.int32),
            pltpu.SMEM((GROUPS, 1, 128), jnp.int32),
            pltpu.VMEM((TENSOR, 8, PACK, 128), bf16),
            pltpu.VMEM((TENSOR, 8, PACK, 128), bf16),
            pltpu.VMEM((TENSOR, 256, D), bf16),
            pltpu.VMEM((TENSOR, D, D), bf16),
            pltpu.VMEM((TENSOR, D, D), bf16),
            pltpu.VMEM((1, 128), f32),
            pltpu.VMEM((2, TENSOR, 1, 128), f32),
            pltpu.VMEM((1, 128), f32),
            pltpu.VMEM((GROUPS, 1, 128), f32),
            dma((5,)),
            dma((GROUPS,)), dma((GROUPS,)),
            dma((GROUPS,)), dma((GROUPS,)),
            dma((GROUPS,)), dma((GROUPS,)),
            dma((TENSOR,)), dma((TENSOR,)),
            dma((3,)), dma((3, 8)), dma((3, 8)),
            dma((2, TENSOR)), dma((2, TENSOR)),
            dma((GROUPS,)), dma((GROUPS,)),
            dma, dma,
        ],
        compiler_params=pltpu.CompilerParams(
            collective_id=0, has_side_effects=True, vmem_limit_bytes=56 * 1024 * 1024
        ),
    )(
        pair_source.reshape(1, PAIRS), pair_image.reshape(1, PAIRS), w_match, states,
        jnp.transpose(patches[0, 0], (1, 0, 2)), w_query.T, w_key.T, w_value.T, w_out, w_in, w_down,
    )


def solution(mesh):
    placed = (
        P("query", "owner", None, None, None),
        P(("query", "owner"), None, None),
        P(("query", "owner"), None),
        P(("query", "owner")),
        P(None, "tensor"),
        P(None, "tensor"),
        P(None, "tensor"),
        P("tensor", None),
        P(None, "tensor"),
        P("tensor", None),
        P(),
    )
    return jax.shard_map(
        body, mesh=mesh, in_specs=placed, out_specs=P(None, "owner"), check_vma=False
    )
```

```python
import functools

import jax
import jax.numpy as jnp
from jax import lax
from jax.experimental import pallas as pl
from jax.experimental.pallas import tpu as pltpu
from jax.sharding import PartitionSpec as P

D = 768
PATCH = 257
VIS = 1408
PAIRS = 32
NQ = 32
IMAGES = 8
SLOTS = 2
NX, NZ = 4, 8
GROUPS = NX * NZ
TENSOR = 4
PACK = 48
KEYS = 384
ROWS = PAIRS // TENSOR * NQ
EPSILON = 1e-06
MESH = pl.DeviceIdType.MESH
bf16, f32 = jnp.bfloat16, jnp.float32


def kernel(
    source, image, match_ref, states_h, patches_h, wq_h, wk_h, wv_h, wout_h, win_h, wdn_h,
    out_ref,
    states, patches, wqx, wkvx, both, img, idx_v, idx,
    qpk, qsend, qrecv, csend, crecv, keys, values, img_recv, img_s,
    ysend, yrecv, wout, win, wdn, fsend, frecv, osend, orecv,
    load_sem, img_ss, img_rs, q_ss, q_rs, c_ss, c_rs, y_ss, y_rs,
    w_own, w_ss, w_rs, f_ss, f_rs, o_ss, o_rs, img_sem, idx_sem,
):
    me = lax.axis_index("query")
    core = lax.axis_index("owner")
    ty = lax.axis_index("tensor")
    x, z = lax.div(me, NZ), lax.rem(me, NZ)

    def step(i):
        return lax.div(i + 1, 2) * (2 * lax.rem(i, 2) - 1)

    def peer(k):
        return lax.rem(x + step(lax.rem(k, NX)) + NX, NX) * NZ + lax.rem(z + step(lax.div(k, NX)) + NZ, NZ)

    steps = [((i + 1) // 2) * (2 * (i % 2) - 1) for i in range(NZ)]
    columns = [lax.rem(x + steps[i] + NX, NX) * NZ for i in range(NX)]
    rows_z = [lax.rem(z + steps[i] + NZ, NZ) for i in range(NZ)]
    peers = [columns[k % NX] + rows_z[k // NX] for k in range(GROUPS)]
    others = peers[1:]

    def y_peer(k):
        return lax.rem(ty + k, TENSOR)

    def remote(src, dst, ss, rs, **device):
        return pltpu.make_async_remote_copy(
            src_ref=src, dst_ref=dst, send_sem=ss, recv_sem=rs, device_id=device, device_id_type=MESH
        )

    loads = [
        pltpu.make_async_copy(src, dst, load_sem.at[i])
        for i, (src, dst) in enumerate(
            (
                (states_h, states),
                (wq_h, wqx.at[pl.ds(0, 192)]),
                (wk_h, wkvx.at[pl.ds(0, 192)]),
                (wv_h, wkvx.at[pl.ds(256, 192)]),
                (patches_h, patches),
            )
        )
    ]
    for copy in loads[:2]:
        copy.start()

    barrier = pltpu.get_barrier_semaphore()

    for p in reversed(others):
        pl.semaphore_signal(barrier, inc=1, device_id={"query": p}, device_id_type=MESH)

    for k in range(1, TENSOR):
        pl.semaphore_signal(barrier, inc=1, device_id={"tensor": y_peer(k)}, device_id_type=MESH)
    for k in range(TENSOR):
        pl.semaphore_signal(barrier, inc=1, device_id={"owner": 1 - core, "tensor": y_peer(k)}, device_id_type=MESH)

    wide = (PAIRS, 128)
    lanes = lax.broadcasted_iota(jnp.int32, wide, 1)
    number = lax.broadcasted_iota(jnp.int32, wide, 0)

    def row_of(v):
        return jnp.sum(v, axis=0, keepdims=True)

    def column_of(v):
        return jnp.sum(jnp.where(lanes == number, v, 0), axis=1, keepdims=True)

    source_row = jnp.concatenate([source[...], jnp.full((1, 128 - PAIRS), -1, jnp.int32)], axis=1)
    image_row = jnp.concatenate([image[...], jnp.zeros((1, 128 - PAIRS), jnp.int32)], axis=1)
    earlier = (column_of(source_row) == source_row) & (number < lanes)
    slot_row = source_row * SLOTS + row_of(earlier.astype(jnp.int32))
    placed = column_of(slot_row) == lanes
    img[...] = row_of(jnp.where(placed, column_of(image_row), 0))
    idx_v[0:1] = row_of(jnp.where(placed, number, 0))
    idx_v[1:2] = slot_row
    to_index = pltpu.make_async_copy(idx_v, idx, idx_sem)
    to_index.start()

    loads[0].wait()
    loads[1].wait()
    for copy in loads[2:]:
        copy.start()
    wqx[192:256] = wqx[128:192]
    low = lax.broadcasted_iota(jnp.int32, (1, 128), 1) < 64

    def times(a, b):
        return lax.dot_general(a, b, (((1,), (1,)), ((), ())), preferred_element_type=f32)

    q = times(states[...].reshape(PAIRS * NQ, D), wqx[...]).reshape(PAIRS, NQ, 256)
    last = jnp.where(low[None], q[:, :16, 128:], q[:, 16:, 128:])
    qpk[...] = jnp.concatenate([q[:, :, :128], last], axis=1).astype(bf16)

    pl.semaphore_wait(barrier, GROUPS - 1 + 2 * TENSOR - 1)
    to_index.wait()

    right, left, across = y_peer(1), y_peer(3), y_peer(2)
    shards = ((wout_h, wout, 192), (win_h, win, D), (wdn_h, wdn, D))

    def part(ref, t, size, begin, length):
        return ref.at[t, pl.ds(begin, length)]

    def own(i):
        src, dst, size = shards[i]
        return pltpu.make_async_copy(src, dst.at[ty, pl.ds(0, size)], w_own.at[i])

    def first_hop(i, to_right):
        src, dst, size = shards[i]
        begin = pl.multiple_of(core * (size // 2), size // 2)
        j = 0 if to_right else 1
        return remote(
            src.at[pl.ds(begin, size // 2)], dst.at[ty, pl.ds(begin, size // 2)],
            w_ss.at[i, j], w_rs.at[i, j], tensor=right if to_right else left,
        )

    def second_hop(i, to_right, receive=False):
        _, dst, size = shards[i]
        quarter = size // 4
        t = across if receive else (left if to_right else right)
        begin = pl.multiple_of(core * (size // 2) + (0 if to_right else quarter), quarter)
        place = dst.at[t, pl.ds(begin, quarter)]
        j = 2 if to_right else 3
        return remote(place, place, w_ss.at[i, j], w_rs.at[i, j], tensor=right if to_right else left)

    def sibling(i, which, receive=False):
        _, dst, size = shards[i]
        c = 1 - core if receive else core
        quarter = size // 4
        if which < 2:
            t, begin, length = (left if which == 0 else right), c * (size // 2), size // 2
        else:
            t, begin, length = across, c * (size // 2) + (which - 2) * quarter, quarter
        place = dst.at[t, pl.ds(pl.multiple_of(begin, quarter), length)]
        return remote(place, place, w_ss.at[i, 4 + which], w_rs.at[i, 4 + which], owner=1 - core)

    def weights_0(i):
        own(i).start()
        first_hop(i, True).start()
        first_hop(i, False).start()

    def weights_1(i):
        first_hop(i, True).wait_recv()
        second_hop(i, True).start()
        sibling(i, 0).start()
        first_hop(i, False).wait_recv()
        second_hop(i, False).start()
        sibling(i, 1).start()

    def weights_2(i):
        second_hop(i, True, True).wait_recv()
        sibling(i, 2).start()
        second_hop(i, False, True).wait_recv()
        sibling(i, 3).start()

    def weights_3(i):
        for which in range(4):
            sibling(i, which, True).wait_recv()
        own(i).wait()

    for i in range(3):
        weights_0(i)

    def img_copy(dst, src):
        return remote(img, img_recv.at[src], img_ss.at[dst], img_rs.at[src], query=dst)

    for p in others:
        img_copy(p, me).start()

    def of(ref, p):
        return ref.at[pl.ds(p * SLOTS, SLOTS)]

    def q_copy(dst, src):
        return remote(of(qsend, dst), of(qrecv, src), q_ss.at[dst], q_rs.at[src], query=dst)

    def c_copy(dst, src):
        return remote(of(csend, dst), of(crecv, src), c_ss.at[dst], c_rs.at[src], query=dst)

    for k, p in enumerate(peers):
        for s in range(SLOTS):
            qsend[p * SLOTS + s] = qpk[idx[0, p * SLOTS + s]]
        if k:
            q_copy(p, me).start()

    for copy in loads[2:]:
        copy.wait()
    wkvx[192:256] = wkvx[128:192]
    wkvx[448:512] = wkvx[384:448]

    @pl.loop(0, 4)
    def _(i):
        rows = patches[pl.ds(i * 64, 64)].reshape(512, VIS)
        result = times(rows, wkvx[...])
        for c in range(4):
            both[c, pl.ds(i * 512, 512)] = result[:, c * 128 : c * 128 + 128]

    result = times(patches[256], wkvx[...])
    for c in range(4):
        both[c, 2048:2056] = result[:, c * 128 : c * 128 + 128]

    @pl.loop(0, IMAGES)
    def _(i):
        pad = jnp.zeros((KEYS - 256, 256), bf16)
        keys[i, 256:KEYS] = pad
        values[i, 256:KEYS] = pad
        for c in range(4):
            ref = keys if c < 2 else values
            part = both[c, pl.ds(i, PATCH, stride=IMAGES)].astype(bf16)
            ref[i, 0:PATCH, (c % 2) * 128 : (c % 2) * 128 + 128] = part

    img_recv[me] = img[...]

    for p in others:
        img_copy(p, p).wait_recv()

    to_scalars = pltpu.make_async_copy(img_recv, img_s, img_sem)
    to_scalars.start()
    to_scalars.wait()

    first_mask = low.astype(f32).astype(bf16)
    second_mask = (1 - low.astype(f32)).astype(bf16)
    column = lax.broadcasted_iota(jnp.int32, (1, KEYS), 1)

    factor = 0.125 * 1.4426950408889634

    def attend(slots, images):
        scores, weights, context, packed = [], [], [], []
        for slot, image in zip(slots, images):
            rows = qrecv[slot]
            a, b = rows[0:32], rows[32:48]
            top = jnp.concatenate([a * first_mask, a * second_mask, jnp.zeros((32, 128), bf16)], axis=0)
            bottom = jnp.concatenate([jnp.zeros((64, 128), bf16), b * first_mask, b * second_mask], axis=0)
            scores.append(times(jnp.concatenate([top, bottom], axis=1), keys[image]))
        for s in scores:
            s = jnp.where(column < PATCH, s, -jnp.inf)
            e = jnp.exp2((s - jnp.max(s, axis=1, keepdims=True)) * factor)
            weights.append((e * (1.0 / jnp.sum(e, axis=1, keepdims=True))).astype(bf16))
        for w, image in zip(weights, images):
            context.append(jnp.dot(w, values[image], preferred_element_type=f32))
        for c in context:
            c01 = jnp.where(low, c[0:32, :128], c[32:64, :128])
            c2 = jnp.where(low, c[64:80, 128:], c[80:96, 128:])
            packed.append(jnp.concatenate([c01, c2], axis=0).astype(bf16))
        return packed

    qrecv[pl.ds(me * SLOTS, SLOTS)] = qsend[pl.ds(me * SLOTS, SLOTS)]

    @pl.loop(0, GROUPS // NX)
    def _(n):
        four = [peer(n * NX + i) for i in range(NX)]
        for i, p in enumerate(four):
            if i:
                q_copy(p, p).wait_recv()
            else:
                pl.when(n > 0)(q_copy(p, p).wait_recv)
        for i in range(3):

            @pl.when(n == GROUPS // NX - 3 + i)
            def _():
                weights_1(i)

        slots = [p * SLOTS + s for p in four for s in range(SLOTS)]
        images = [img_s[p, 0, me * SLOTS + s] for p in four for s in range(SLOTS)]
        for slot, rows in zip(slots, attend(slots, images)):
            csend[slot] = rows
        for i, p in enumerate(four):
            if i:
                c_copy(p, me).start()
            else:
                pl.when(n > 0)(c_copy(p, me).start)

    crecv[pl.ds(me * SLOTS, SLOTS)] = csend[pl.ds(me * SLOTS, SLOTS)]

    for p in others:
        img_copy(p, p).wait_send()
        q_copy(p, p).wait_send()
        c_copy(p, p).wait_recv()

    def y_copy(dst, src):
        return remote(ysend.at[dst], yrecv.at[src], y_ss.at[dst], y_rs.at[src], tensor=dst)

    for k in (2, 1, 3):
        t = y_peer(k)
        for j in range(8):
            ysend[t, j] = crecv[idx[1, t * 8 + j]]
        y_copy(t, ty).start()
    for j in range(8):
        yrecv[ty, j] = crecv[idx[1, ty * 8 + j]]

    for p in others:
        c_copy(p, p).wait_send()

    for i in range(3):
        weights_2(i)
    weights_3(0)
    for t in range(TENSOR):
        wout[t, 192:256] = wout[t, 128:192]
    def norm(v):
        mean = jnp.mean(v, axis=-1, keepdims=True)
        squares = jnp.mean(v * v, axis=-1, keepdims=True)
        return (v - mean) * lax.rsqrt(squares - mean * mean + EPSILON)

    total = states[pl.ds(ty * 8, 8)].reshape(ROWS, D).astype(f32)
    for k in (0, 1, 3, 2):
        t = y_peer(k)
        if k:
            y_copy(t, t).wait_recv()
        c = yrecv[t]
        b = c[:, 32:]
        second = jnp.concatenate([b * first_mask[None], b * second_mask[None]], axis=1)
        rows = jnp.concatenate([c[:, :32], second], axis=2).reshape(ROWS, 256)
        total = total + jnp.dot(rows, wout[t], preferred_element_type=f32)
    first_norm = norm(total).astype(bf16)

    weights_3(1)
    weights_3(2)
    total = first_norm.astype(f32)

    def up(t):
        return jnp.dot(first_norm, win[t], preferred_element_type=f32)

    later = up(0)
    for t in range(TENSOR):
        now = later
        if t < TENSOR - 1:
            later = up(t + 1)
        hidden = (0.5 * now * (1.0 + lax.erf(now * 0.7071067811865476))).astype(bf16)
        total = total + jnp.dot(hidden, wdn[t], preferred_element_type=f32)
    score = jnp.sum(norm(total) * match_ref[...].astype(f32).reshape(1, D), axis=-1, keepdims=True)
    score = jnp.mean(score.reshape(8, NQ, 1), axis=1)

    lane = lax.broadcasted_iota(jnp.int32, (8, 128), 1)
    pair = lax.broadcasted_iota(jnp.int32, (8, 128), 0) + (core * PAIRS + ty * 8)
    row = jnp.sum(jnp.where(lane == pair, score, 0.0), axis=0, keepdims=True)
    fsend[...] = row
    frecv[core, ty] = row
    group = [(c, k) for c in (0, 1) for k in range(TENSOR) if c or k]

    def f_copy(c, k, receive=False):
        device = {"owner": lax.rem(core + c, 2), "tensor": y_peer(k)}
        at = (device["owner"], device["tensor"]) if receive else (core, ty)
        return remote(fsend, frecv.at[at], f_ss.at[c, k], f_rs.at[at], **device)

    for c, k in reversed(group):
        f_copy(c, k).start()
    for c, k in group:
        f_copy(c, k, True).wait_recv()
    row = jnp.sum(frecv[...].reshape(2 * TENSOR, 128), axis=0, keepdims=True)
    valid = lax.broadcasted_iota(jnp.int32, (1, 128), 1) < 2 * PAIRS
    partition = jnp.sum(jnp.where(valid, jnp.exp(row), 0.0), axis=1, keepdims=True)
    row = row - jnp.log(partition)
    row = jnp.where(core == 0, row, pltpu.roll(row, 128 - PAIRS, 1))
    osend[...] = row
    orecv[me] = row

    def o_copy(dst, src):
        return remote(osend, orecv.at[src], o_ss.at[dst], o_rs.at[src], query=dst)

    for p in reversed(others):
        o_copy(p, me).start()

    for k in range(1, TENSOR):
        t = y_peer(k)
        y_copy(t, t).wait_send()
    for c, k in group:
        f_copy(c, k).wait_send()
    for i in range(3):
        first_hop(i, True).wait_send()
        first_hop(i, False).wait_send()
        second_hop(i, True).wait_send()
        second_hop(i, False).wait_send()
        for which in range(4):
            sibling(i, which).wait_send()
    for p in others:
        o_copy(p, p).wait_send()

    for p in others:
        o_copy(p, p).wait_recv()

    out_ref[...] = orecv[...].reshape(GROUPS, 128)[:, :PAIRS]


def body(
    patches, states, pair_source, pair_image, w_query, w_key, w_value, w_out, w_in, w_down, w_match
):
    vmem = pl.BlockSpec(memory_space=pltpu.VMEM)
    hbm = pl.BlockSpec(memory_space=pl.ANY)
    dma = pltpu.SemaphoreType.DMA
    return pl.pallas_call(
        kernel,
        out_shape=jax.ShapeDtypeStruct((GROUPS, PAIRS), f32),
        in_specs=[vmem] * 3 + [hbm] * 8,
        out_specs=vmem,
        scratch_shapes=[
            pltpu.VMEM((PAIRS, NQ, D), bf16),
            pltpu.VMEM((PATCH, IMAGES, VIS), bf16),
            pltpu.VMEM((256, D), bf16),
            pltpu.VMEM((512, VIS), bf16),
            pltpu.VMEM((4, PATCH * IMAGES, 128), f32),
            pltpu.VMEM((1, 128), jnp.int32),
            pltpu.VMEM((2, 128), jnp.int32),
            pltpu.SMEM((2, 128), jnp.int32),
            pltpu.VMEM((PAIRS, PACK, 128), bf16),
            pltpu.VMEM((GROUPS * SLOTS, PACK, 128), bf16),
            pltpu.VMEM((GROUPS * SLOTS, PACK, 128), bf16),
            pltpu.VMEM((GROUPS * SLOTS, PACK, 128), bf16),
            pltpu.VMEM((GROUPS * SLOTS, PACK, 128), bf16),
            pltpu.VMEM((IMAGES, KEYS, 256), bf16),
            pltpu.VMEM((IMAGES, KEYS, 256), bf16),
            pltpu.VMEM((GROUPS, 1, 128), jnp.int32),
            pltpu.SMEM((GROUPS, 1, 128), jnp.int32),
            pltpu.VMEM((TENSOR, 8, PACK, 128), bf16),
            pltpu.VMEM((TENSOR, 8, PACK, 128), bf16),
            pltpu.VMEM((TENSOR, 256, D), bf16),
            pltpu.VMEM((TENSOR, D, D), bf16),
            pltpu.VMEM((TENSOR, D, D), bf16),
            pltpu.VMEM((1, 128), f32),
            pltpu.VMEM((2, TENSOR, 1, 128), f32),
            pltpu.VMEM((1, 128), f32),
            pltpu.VMEM((GROUPS, 1, 128), f32),
            dma((5,)),
            dma((GROUPS,)), dma((GROUPS,)),
            dma((GROUPS,)), dma((GROUPS,)),
            dma((GROUPS,)), dma((GROUPS,)),
            dma((TENSOR,)), dma((TENSOR,)),
            dma((3,)), dma((3, 8)), dma((3, 8)),
            dma((2, TENSOR)), dma((2, TENSOR)),
            dma((GROUPS,)), dma((GROUPS,)),
            dma, dma,
        ],
        compiler_params=pltpu.CompilerParams(
            collective_id=0, has_side_effects=True, vmem_limit_bytes=56 * 1024 * 1024
        ),
    )(
        pair_source.reshape(1, PAIRS), pair_image.reshape(1, PAIRS), w_match, states,
        jnp.transpose(patches[0, 0], (1, 0, 2)), w_query.T, w_key.T, w_value.T, w_out, w_in, w_down,
    )


def solution(mesh):
    placed = (
        P("query", "owner", None, None, None),
        P(("query", "owner"), None, None),
        P(("query", "owner"), None),
        P(("query", "owner")),
        P(None, "tensor"),
        P(None, "tensor"),
        P(None, "tensor"),
        P("tensor", None),
        P(None, "tensor"),
        P("tensor", None),
        P(),
    )
    return jax.shard_map(
        body, mesh=mesh, in_specs=placed, out_specs=P(None, "owner"), check_vma=False
    )
```

```python
import functools

import jax
import jax.numpy as jnp
from jax import lax
from jax.experimental import pallas as pl
from jax.experimental.pallas import tpu as pltpu
from jax.sharding import PartitionSpec as P

D = 768
PATCH = 257
VIS = 1408
PAIRS = 32
NQ = 32
IMAGES = 8
SLOTS = 2
NX, NZ = 4, 8
GROUPS = NX * NZ
TENSOR = 4
PACK = 48
KEYS = 384
ROWS = PAIRS // TENSOR * NQ
EPSILON = 1e-06
MESH = pl.DeviceIdType.MESH
bf16, f32 = jnp.bfloat16, jnp.float32


def kernel(
    source_h, image_h, match_h, states_h, patches_h, wq_h, wk_h, wv_h, wout_h, win_h, wdn_h,
    out_ref,
    source, image, match_ref, states, patches, wqx, wkvx, both, img, idx_v, idx,
    qpk, qsend, qrecv, csend, crecv, keys, values, img_recv, img_s,
    ysend, yrecv, wout, win, wdn, fsend, frecv, osend, orecv,
    small_sem, load_sem, img_ss, img_rs, q_ss, q_rs, c_ss, c_rs, y_ss, y_rs,
    w_own, w_ss, w_rs, f_ss, f_rs, o_ss, o_rs, img_sem, idx_sem,
):
    me = lax.axis_index("query")
    core = lax.axis_index("owner")
    ty = lax.axis_index("tensor")
    x, z = lax.div(me, NZ), lax.rem(me, NZ)

    def step(i):
        return lax.div(i + 1, 2) * (2 * lax.rem(i, 2) - 1)

    def peer(k):
        return lax.rem(x + step(lax.rem(k, NX)) + NX, NX) * NZ + lax.rem(z + step(lax.div(k, NX)) + NZ, NZ)

    steps = [((i + 1) // 2) * (2 * (i % 2) - 1) for i in range(NZ)]
    columns = [lax.rem(x + steps[i] + NX, NX) * NZ for i in range(NX)]
    rows_z = [lax.rem(z + steps[i] + NZ, NZ) for i in range(NZ)]
    peers = [columns[k % NX] + rows_z[k // NX] for k in range(GROUPS)]
    others = peers[1:]

    def y_peer(k):
        return lax.rem(ty + k, TENSOR)

    def remote(src, dst, ss, rs, **device):
        return pltpu.make_async_remote_copy(
            src_ref=src, dst_ref=dst, send_sem=ss, recv_sem=rs, device_id=device, device_id_type=MESH
        )

    loads = [
        pltpu.make_async_copy(src, dst, load_sem.at[i])
        for i, (src, dst) in enumerate(
            (
                (states_h, states),
                (wq_h, wqx.at[pl.ds(0, 192)]),
                (wk_h, wkvx.at[pl.ds(0, 192)]),
                (wv_h, wkvx.at[pl.ds(256, 192)]),
                (patches_h, patches),
            )
        )
    ]
    small = [
        pltpu.make_async_copy(src, dst, small_sem.at[i])
        for i, (src, dst) in enumerate(((source_h, source), (image_h, image), (match_h, match_ref)))
    ]
    for copy in small + loads[:2]:
        copy.start()

    barrier = pltpu.get_barrier_semaphore()

    for p in reversed(others):
        pl.semaphore_signal(barrier, inc=1, device_id={"query": p}, device_id_type=MESH)

    for k in range(1, TENSOR):
        pl.semaphore_signal(barrier, inc=1, device_id={"tensor": y_peer(k)}, device_id_type=MESH)
    for k in range(TENSOR):
        pl.semaphore_signal(barrier, inc=1, device_id={"owner": 1 - core, "tensor": y_peer(k)}, device_id_type=MESH)

    wide = (PAIRS, 128)
    lanes = lax.broadcasted_iota(jnp.int32, wide, 1)
    number = lax.broadcasted_iota(jnp.int32, wide, 0)

    def row_of(v):
        return jnp.sum(v, axis=0, keepdims=True)

    def column_of(v):
        return jnp.sum(jnp.where(lanes == number, v, 0), axis=1, keepdims=True)

    for copy in small:
        copy.wait()
    source_row = jnp.concatenate([source[...], jnp.full((1, 128 - PAIRS), -1, jnp.int32)], axis=1)
    image_row = jnp.concatenate([image[...], jnp.zeros((1, 128 - PAIRS), jnp.int32)], axis=1)
    earlier = (column_of(source_row) == source_row) & (number < lanes)
    slot_row = source_row * SLOTS + row_of(earlier.astype(jnp.int32))
    placed = column_of(slot_row) == lanes
    img[...] = row_of(jnp.where(placed, column_of(image_row), 0))
    idx_v[0:1] = row_of(jnp.where(placed, number, 0))
    idx_v[1:2] = slot_row
    to_index = pltpu.make_async_copy(idx_v, idx, idx_sem)
    to_index.start()

    loads[0].wait()
    loads[1].wait()
    for copy in loads[2:]:
        copy.start()
    wqx[192:256] = wqx[128:192]
    low = lax.broadcasted_iota(jnp.int32, (1, 128), 1) < 64

    def times(a, b):
        return lax.dot_general(a, b, (((1,), (1,)), ((), ())), preferred_element_type=f32)

    q = times(states[...].reshape(PAIRS * NQ, D), wqx[...]).reshape(PAIRS, NQ, 256)
    last = jnp.where(low[None], q[:, :16, 128:], q[:, 16:, 128:])
    qpk[...] = jnp.concatenate([q[:, :, :128], last], axis=1).astype(bf16)

    pl.semaphore_wait(barrier, GROUPS - 1 + 2 * TENSOR - 1)
    to_index.wait()

    right, left, across = y_peer(1), y_peer(3), y_peer(2)
    shards = ((wout_h, wout, 192), (win_h, win, D), (wdn_h, wdn, D))

    def part(ref, t, size, begin, length):
        return ref.at[t, pl.ds(begin, length)]

    def own(i):
        src, dst, size = shards[i]
        return pltpu.make_async_copy(src, dst.at[ty, pl.ds(0, size)], w_own.at[i])

    def first_hop(i, to_right):
        src, dst, size = shards[i]
        begin = pl.multiple_of(core * (size // 2), size // 2)
        j = 0 if to_right else 1
        return remote(
            src.at[pl.ds(begin, size // 2)], dst.at[ty, pl.ds(begin, size // 2)],
            w_ss.at[i, j], w_rs.at[i, j], tensor=right if to_right else left,
        )

    def second_hop(i, to_right, receive=False):
        _, dst, size = shards[i]
        quarter = size // 4
        t = across if receive else (left if to_right else right)
        begin = pl.multiple_of(core * (size // 2) + (0 if to_right else quarter), quarter)
        place = dst.at[t, pl.ds(begin, quarter)]
        j = 2 if to_right else 3
        return remote(place, place, w_ss.at[i, j], w_rs.at[i, j], tensor=right if to_right else left)

    def sibling(i, which, receive=False):
        _, dst, size = shards[i]
        c = 1 - core if receive else core
        quarter = size // 4
        if which < 2:
            t, begin, length = (left if which == 0 else right), c * (size // 2), size // 2
        else:
            t, begin, length = across, c * (size // 2) + (which - 2) * quarter, quarter
        place = dst.at[t, pl.ds(pl.multiple_of(begin, quarter), length)]
        return remote(place, place, w_ss.at[i, 4 + which], w_rs.at[i, 4 + which], owner=1 - core)

    def weights_0(i):
        own(i).start()
        first_hop(i, True).start()
        first_hop(i, False).start()

    def weights_1(i):
        first_hop(i, True).wait_recv()
        second_hop(i, True).start()
        sibling(i, 0).start()
        first_hop(i, False).wait_recv()
        second_hop(i, False).start()
        sibling(i, 1).start()

    def weights_2(i):
        second_hop(i, True, True).wait_recv()
        sibling(i, 2).start()
        second_hop(i, False, True).wait_recv()
        sibling(i, 3).start()

    def weights_3(i):
        for which in range(4):
            sibling(i, which, True).wait_recv()
        own(i).wait()

    for i in range(3):
        weights_0(i)

    def img_copy(dst, src):
        return remote(img, img_recv.at[src], img_ss.at[dst], img_rs.at[src], query=dst)

    for p in others:
        img_copy(p, me).start()

    def of(ref, p):
        return ref.at[pl.ds(p * SLOTS, SLOTS)]

    def q_copy(dst, src):
        return remote(of(qsend, dst), of(qrecv, src), q_ss.at[dst], q_rs.at[src], query=dst)

    def c_copy(dst, src):
        return remote(of(csend, dst), of(crecv, src), c_ss.at[dst], c_rs.at[src], query=dst)

    for k, p in enumerate(peers):
        for s in range(SLOTS):
            qsend[p * SLOTS + s] = qpk[idx[0, p * SLOTS + s]]
        if k:
            q_copy(p, me).start()

    for copy in loads[2:]:
        copy.wait()
    wkvx[192:256] = wkvx[128:192]
    wkvx[448:512] = wkvx[384:448]

    @pl.loop(0, 4)
    def _(i):
        rows = patches[pl.ds(i * 64, 64)].reshape(512, VIS)
        result = times(rows, wkvx[...])
        for c in range(4):
            both[c, pl.ds(i * 512, 512)] = result[:, c * 128 : c * 128 + 128]

    result = times(patches[256], wkvx[...])
    for c in range(4):
        both[c, 2048:2056] = result[:, c * 128 : c * 128 + 128]

    @pl.loop(0, IMAGES)
    def _(i):
        pad = jnp.zeros((KEYS - 256, 256), bf16)
        keys[i, 256:KEYS] = pad
        values[i, 256:KEYS] = pad
        for c in range(4):
            ref = keys if c < 2 else values
            part = both[c, pl.ds(i, PATCH, stride=IMAGES)].astype(bf16)
            ref[i, 0:PATCH, (c % 2) * 128 : (c % 2) * 128 + 128] = part

    img_recv[me] = img[...]

    for p in others:
        img_copy(p, p).wait_recv()

    to_scalars = pltpu.make_async_copy(img_recv, img_s, img_sem)
    to_scalars.start()
    to_scalars.wait()

    first_mask = low.astype(f32).astype(bf16)
    second_mask = (1 - low.astype(f32)).astype(bf16)
    column = lax.broadcasted_iota(jnp.int32, (1, KEYS), 1)

    factor = 0.125 * 1.4426950408889634

    def attend(slots, images):
        scores, weights, context, packed = [], [], [], []
        for slot, image in zip(slots, images):
            rows = qrecv[slot]
            a, b = rows[0:32], rows[32:48]
            top = jnp.concatenate([a * first_mask, a * second_mask, jnp.zeros((32, 128), bf16)], axis=0)
            bottom = jnp.concatenate([jnp.zeros((64, 128), bf16), b * first_mask, b * second_mask], axis=0)
            scores.append(times(jnp.concatenate([top, bottom], axis=1), keys[image]))
        for s in scores:
            s = jnp.where(column < PATCH, s, -jnp.inf)
            e = jnp.exp2((s - jnp.max(s, axis=1, keepdims=True)) * factor)
            weights.append((e * (1.0 / jnp.sum(e, axis=1, keepdims=True))).astype(bf16))
        for w, image in zip(weights, images):
            context.append(jnp.dot(w, values[image], preferred_element_type=f32))
        for c in context:
            c01 = jnp.where(low, c[0:32, :128], c[32:64, :128])
            c2 = jnp.where(low, c[64:80, 128:], c[80:96, 128:])
            packed.append(jnp.concatenate([c01, c2], axis=0).astype(bf16))
        return packed

    qrecv[pl.ds(me * SLOTS, SLOTS)] = qsend[pl.ds(me * SLOTS, SLOTS)]

    @pl.loop(0, GROUPS // NX)
    def _(n):
        four = [peer(n * NX + i) for i in range(NX)]
        for i, p in enumerate(four):
            if i:
                q_copy(p, p).wait_recv()
            else:
                pl.when(n > 0)(q_copy(p, p).wait_recv)
        for i in range(3):

            @pl.when(n == GROUPS // NX - 3 + i)
            def _():
                weights_1(i)

        slots = [p * SLOTS + s for p in four for s in range(SLOTS)]
        images = [img_s[p, 0, me * SLOTS + s] for p in four for s in range(SLOTS)]
        for slot, rows in zip(slots, attend(slots, images)):
            csend[slot] = rows
        for i, p in enumerate(four):
            if i:
                c_copy(p, me).start()
            else:
                pl.when(n > 0)(c_copy(p, me).start)

    crecv[pl.ds(me * SLOTS, SLOTS)] = csend[pl.ds(me * SLOTS, SLOTS)]

    for p in others:
        img_copy(p, p).wait_send()
        q_copy(p, p).wait_send()
        c_copy(p, p).wait_recv()

    def y_copy(dst, src):
        return remote(ysend.at[dst], yrecv.at[src], y_ss.at[dst], y_rs.at[src], tensor=dst)

    for k in (2, 1, 3):
        t = y_peer(k)
        for j in range(8):
            ysend[t, j] = crecv[idx[1, t * 8 + j]]
        y_copy(t, ty).start()
    for j in range(8):
        yrecv[ty, j] = crecv[idx[1, ty * 8 + j]]

    for p in others:
        c_copy(p, p).wait_send()

    for i in range(3):
        weights_2(i)
    weights_3(0)
    for t in range(TENSOR):
        wout[t, 192:256] = wout[t, 128:192]
    def norm(v):
        mean = jnp.mean(v, axis=-1, keepdims=True)
        squares = jnp.mean(v * v, axis=-1, keepdims=True)
        return (v - mean) * lax.rsqrt(squares - mean * mean + EPSILON)

    total = states[pl.ds(ty * 8, 8)].reshape(ROWS, D).astype(f32)
    for k in (0, 1, 3, 2):
        t = y_peer(k)
        if k:
            y_copy(t, t).wait_recv()
        c = yrecv[t]
        b = c[:, 32:]
        second = jnp.concatenate([b * first_mask[None], b * second_mask[None]], axis=1)
        rows = jnp.concatenate([c[:, :32], second], axis=2).reshape(ROWS, 256)
        total = total + jnp.dot(rows, wout[t], preferred_element_type=f32)
    first_norm = norm(total).astype(bf16)

    weights_3(1)
    weights_3(2)
    total = first_norm.astype(f32)

    def up(t):
        return jnp.dot(first_norm, win[t], preferred_element_type=f32)

    later = up(0)
    for t in range(TENSOR):
        now = later
        if t < TENSOR - 1:
            later = up(t + 1)
        hidden = (0.5 * now * (1.0 + lax.erf(now * 0.7071067811865476))).astype(bf16)
        total = total + jnp.dot(hidden, wdn[t], preferred_element_type=f32)
    score = jnp.sum(norm(total) * match_ref[...].astype(f32).reshape(1, D), axis=-1, keepdims=True)
    score = jnp.mean(score.reshape(8, NQ, 1), axis=1)

    lane = lax.broadcasted_iota(jnp.int32, (8, 128), 1)
    pair = lax.broadcasted_iota(jnp.int32, (8, 128), 0) + (core * PAIRS + ty * 8)
    row = jnp.sum(jnp.where(lane == pair, score, 0.0), axis=0, keepdims=True)
    fsend[...] = row
    frecv[core, ty] = row
    group = [(c, k) for c in (0, 1) for k in range(TENSOR) if c or k]

    def f_copy(c, k, receive=False):
        device = {"owner": lax.rem(core + c, 2), "tensor": y_peer(k)}
        at = (device["owner"], device["tensor"]) if receive else (core, ty)
        return remote(fsend, frecv.at[at], f_ss.at[c, k], f_rs.at[at], **device)

    for c, k in reversed(group):
        f_copy(c, k).start()
    for c, k in group:
        f_copy(c, k, True).wait_recv()
    row = jnp.sum(frecv[...].reshape(2 * TENSOR, 128), axis=0, keepdims=True)
    valid = lax.broadcasted_iota(jnp.int32, (1, 128), 1) < 2 * PAIRS
    partition = jnp.sum(jnp.where(valid, jnp.exp(row), 0.0), axis=1, keepdims=True)
    row = row - jnp.log(partition)
    row = jnp.where(core == 0, row, pltpu.roll(row, 128 - PAIRS, 1))
    osend[...] = row
    orecv[me] = row

    def o_copy(dst, src):
        return remote(osend, orecv.at[src], o_ss.at[dst], o_rs.at[src], query=dst)

    for p in reversed(others):
        o_copy(p, me).start()

    for k in range(1, TENSOR):
        t = y_peer(k)
        y_copy(t, t).wait_send()
    for c, k in group:
        f_copy(c, k).wait_send()
    for i in range(3):
        first_hop(i, True).wait_send()
        first_hop(i, False).wait_send()
        second_hop(i, True).wait_send()
        second_hop(i, False).wait_send()
        for which in range(4):
            sibling(i, which).wait_send()
    for p in others:
        o_copy(p, p).wait_send()

    for p in others:
        o_copy(p, p).wait_recv()

    out_ref[...] = orecv[...].reshape(GROUPS, 128)[:, :PAIRS]


def body(
    patches, states, pair_source, pair_image, w_query, w_key, w_value, w_out, w_in, w_down, w_match
):
    vmem = pl.BlockSpec(memory_space=pltpu.VMEM)
    hbm = pl.BlockSpec(memory_space=pl.ANY)
    dma = pltpu.SemaphoreType.DMA
    return pl.pallas_call(
        kernel,
        out_shape=jax.ShapeDtypeStruct((GROUPS, PAIRS), f32),
        in_specs=[hbm] * 11,
        out_specs=vmem,
        scratch_shapes=[
            pltpu.VMEM((1, PAIRS), jnp.int32),
            pltpu.VMEM((1, PAIRS), jnp.int32),
            pltpu.VMEM((D,), bf16),
            pltpu.VMEM((PAIRS, NQ, D), bf16),
            pltpu.VMEM((PATCH, IMAGES, VIS), bf16),
            pltpu.VMEM((256, D), bf16),
            pltpu.VMEM((512, VIS), bf16),
            pltpu.VMEM((4, PATCH * IMAGES, 128), f32),
            pltpu.VMEM((1, 128), jnp.int32),
            pltpu.VMEM((2, 128), jnp.int32),
            pltpu.SMEM((2, 128), jnp.int32),
            pltpu.VMEM((PAIRS, PACK, 128), bf16),
            pltpu.VMEM((GROUPS * SLOTS, PACK, 128), bf16),
            pltpu.VMEM((GROUPS * SLOTS, PACK, 128), bf16),
            pltpu.VMEM((GROUPS * SLOTS, PACK, 128), bf16),
            pltpu.VMEM((GROUPS * SLOTS, PACK, 128), bf16),
            pltpu.VMEM((IMAGES, KEYS, 256), bf16),
            pltpu.VMEM((IMAGES, KEYS, 256), bf16),
            pltpu.VMEM((GROUPS, 1, 128), jnp.int32),
            pltpu.SMEM((GROUPS, 1, 128), jnp.int32),
            pltpu.VMEM((TENSOR, 8, PACK, 128), bf16),
            pltpu.VMEM((TENSOR, 8, PACK, 128), bf16),
            pltpu.VMEM((TENSOR, 256, D), bf16),
            pltpu.VMEM((TENSOR, D, D), bf16),
            pltpu.VMEM((TENSOR, D, D), bf16),
            pltpu.VMEM((1, 128), f32),
            pltpu.VMEM((2, TENSOR, 1, 128), f32),
            pltpu.VMEM((1, 128), f32),
            pltpu.VMEM((GROUPS, 1, 128), f32),
            dma((3,)), dma((5,)),
            dma((GROUPS,)), dma((GROUPS,)),
            dma((GROUPS,)), dma((GROUPS,)),
            dma((GROUPS,)), dma((GROUPS,)),
            dma((TENSOR,)), dma((TENSOR,)),
            dma((3,)), dma((3, 8)), dma((3, 8)),
            dma((2, TENSOR)), dma((2, TENSOR)),
            dma((GROUPS,)), dma((GROUPS,)),
            dma, dma,
        ],
        compiler_params=pltpu.CompilerParams(
            collective_id=0, has_side_effects=True, vmem_limit_bytes=56 * 1024 * 1024
        ),
    )(
        pair_source.reshape(1, PAIRS), pair_image.reshape(1, PAIRS), w_match, states,
        jnp.transpose(patches[0, 0], (1, 0, 2)), w_query.T, w_key.T, w_value.T, w_out, w_in, w_down,
    )


def solution(mesh):
    placed = (
        P("query", "owner", None, None, None),
        P(("query", "owner"), None, None),
        P(("query", "owner"), None),
        P(("query", "owner")),
        P(None, "tensor"),
        P(None, "tensor"),
        P(None, "tensor"),
        P("tensor", None),
        P(None, "tensor"),
        P("tensor", None),
        P(),
    )
    return jax.shard_map(
        body, mesh=mesh, in_specs=placed, out_specs=P(None, "owner"), check_vma=False
    )
```

```python
import functools

import jax
import jax.numpy as jnp
from jax import lax
from jax.experimental import pallas as pl
from jax.experimental.pallas import tpu as pltpu
from jax.sharding import PartitionSpec as P

D = 768
PATCH = 257
VIS = 1408
PAIRS = 32
NQ = 32
IMAGES = 8
SLOTS = 2
NX, NZ = 4, 8
GROUPS = NX * NZ
TENSOR = 4
PACK = 48
KEYS = 384
ROWS = PAIRS // TENSOR * NQ
EPSILON = 1e-06
MESH = pl.DeviceIdType.MESH
bf16, f32 = jnp.bfloat16, jnp.float32


def kernel(
    source_h, image_h, match_h, states_h, patches_h, wq_h, wk_h, wv_h, wout_h, win_h, wdn_h,
    out_ref,
    source, image, match_ref, states, patches, wqx, wkvx, both, img, idx_v, idx,
    qpk, qsend, qrecv, csend, crecv, keys, values, img_recv, img_s,
    ysend, yrecv, wout, win, wdn, fsend, frecv, osend, orecv,
    small_sem, load_sem, img_ss, img_rs, q_ss, q_rs, c_ss, c_rs, y_ss, y_rs,
    w_own, w_ss, w_rs, f_ss, f_rs, o_ss, o_rs, img_sem, idx_sem,
):
    me = lax.axis_index("query")
    core = lax.axis_index("owner")
    ty = lax.axis_index("tensor")
    x, z = lax.div(me, NZ), lax.rem(me, NZ)

    def step(i):
        return lax.div(i + 1, 2) * (2 * lax.rem(i, 2) - 1)

    def peer(k):
        return lax.rem(x + step(lax.rem(k, NX)) + NX, NX) * NZ + lax.rem(z + step(lax.div(k, NX)) + NZ, NZ)

    steps = [((i + 1) // 2) * (2 * (i % 2) - 1) for i in range(NZ)]
    columns = [lax.rem(x + steps[i] + NX, NX) * NZ for i in range(NX)]
    rows_z = [lax.rem(z + steps[i] + NZ, NZ) for i in range(NZ)]
    peers = [columns[k % NX] + rows_z[k // NX] for k in range(GROUPS)]
    others = peers[1:]

    def y_peer(k):
        return lax.rem(ty + k, TENSOR)

    def remote(src, dst, ss, rs, **device):
        return pltpu.make_async_remote_copy(
            src_ref=src, dst_ref=dst, send_sem=ss, recv_sem=rs, device_id=device, device_id_type=MESH
        )

    loads = [
        pltpu.make_async_copy(src, dst, load_sem.at[i])
        for i, (src, dst) in enumerate(
            (
                (states_h, states),
                (wq_h, wqx.at[pl.ds(0, 192)]),
                (wk_h, wkvx.at[pl.ds(0, 192)]),
                (wv_h, wkvx.at[pl.ds(256, 192)]),
                (patches_h, patches),
            )
        )
    ]
    small = [
        pltpu.make_async_copy(src, dst, small_sem.at[i])
        for i, (src, dst) in enumerate(((source_h, source), (image_h, image), (match_h, match_ref)))
    ]
    for copy in small + loads[:2]:
        copy.start()

    barrier = pltpu.get_barrier_semaphore()

    for p in reversed(others):
        pl.semaphore_signal(barrier, inc=1, device_id={"query": p}, device_id_type=MESH)

    for k in range(1, TENSOR):
        pl.semaphore_signal(barrier, inc=1, device_id={"tensor": y_peer(k)}, device_id_type=MESH)
    for k in range(TENSOR):
        pl.semaphore_signal(barrier, inc=1, device_id={"owner": 1 - core, "tensor": y_peer(k)}, device_id_type=MESH)

    wide = (PAIRS, 128)
    lanes = lax.broadcasted_iota(jnp.int32, wide, 1)
    number = lax.broadcasted_iota(jnp.int32, wide, 0)

    def row_of(v):
        return jnp.sum(v, axis=0, keepdims=True)

    def column_of(v):
        return jnp.sum(jnp.where(lanes == number, v, 0), axis=1, keepdims=True)

    for copy in small:
        copy.wait()
    source_row = jnp.concatenate([source[...], jnp.full((1, 128 - PAIRS), -1, jnp.int32)], axis=1)
    image_row = jnp.concatenate([image[...], jnp.zeros((1, 128 - PAIRS), jnp.int32)], axis=1)
    earlier = (column_of(source_row) == source_row) & (number < lanes)
    slot_row = source_row * SLOTS + row_of(earlier.astype(jnp.int32))
    placed = column_of(slot_row) == lanes
    img[...] = row_of(jnp.where(placed, column_of(image_row), 0))
    idx_v[0:1] = row_of(jnp.where(placed, number, 0))
    idx_v[1:2] = slot_row
    to_index = pltpu.make_async_copy(idx_v, idx, idx_sem)
    to_index.start()

    loads[0].wait()
    loads[1].wait()
    for copy in loads[2:]:
        copy.start()
    wqx[192:256] = wqx[128:192]
    low = lax.broadcasted_iota(jnp.int32, (1, 128), 1) < 64

    def times(a, b):
        return lax.dot_general(a, b, (((1,), (1,)), ((), ())), preferred_element_type=f32)

    q = times(states[...].reshape(PAIRS * NQ, D), wqx[...]).reshape(PAIRS, NQ, 256)
    last = jnp.where(low[None], q[:, :16, 128:], q[:, 16:, 128:])
    qpk[...] = jnp.concatenate([q[:, :, :128], last], axis=1).astype(bf16)

    pl.semaphore_wait(barrier, GROUPS - 1 + 2 * TENSOR - 1)
    to_index.wait()

    right, left, across = y_peer(1), y_peer(3), y_peer(2)
    shards = ((wout_h, wout, 192), (win_h, win, D), (wdn_h, wdn, D))

    def part(ref, t, size, begin, length):
        return ref.at[t, pl.ds(begin, length)]

    def own(i):
        src, dst, size = shards[i]
        return pltpu.make_async_copy(src, dst.at[ty, pl.ds(0, size)], w_own.at[i])

    def first_hop(i, to_right):
        src, dst, size = shards[i]
        begin = pl.multiple_of(core * (size // 2), size // 2)
        j = 0 if to_right else 1
        return remote(
            src.at[pl.ds(begin, size // 2)], dst.at[ty, pl.ds(begin, size // 2)],
            w_ss.at[i, j], w_rs.at[i, j], tensor=right if to_right else left,
        )

    def second_hop(i, to_right, receive=False):
        _, dst, size = shards[i]
        quarter = size // 4
        t = across if receive else (left if to_right else right)
        begin = pl.multiple_of(core * (size // 2) + (0 if to_right else quarter), quarter)
        place = dst.at[t, pl.ds(begin, quarter)]
        j = 2 if to_right else 3
        return remote(place, place, w_ss.at[i, j], w_rs.at[i, j], tensor=right if to_right else left)

    def sibling(i, which, receive=False):
        _, dst, size = shards[i]
        c = 1 - core if receive else core
        quarter = size // 4
        if which < 2:
            t, begin, length = (left if which == 0 else right), c * (size // 2), size // 2
        else:
            t, begin, length = across, c * (size // 2) + (which - 2) * quarter, quarter
        place = dst.at[t, pl.ds(pl.multiple_of(begin, quarter), length)]
        return remote(place, place, w_ss.at[i, 4 + which], w_rs.at[i, 4 + which], owner=1 - core)

    def weights_0(i):
        own(i).start()
        first_hop(i, True).start()
        first_hop(i, False).start()

    def weights_1(i):
        first_hop(i, True).wait_recv()
        second_hop(i, True).start()
        sibling(i, 0).start()
        first_hop(i, False).wait_recv()
        second_hop(i, False).start()
        sibling(i, 1).start()

    def weights_2(i):
        second_hop(i, True, True).wait_recv()
        sibling(i, 2).start()
        second_hop(i, False, True).wait_recv()
        sibling(i, 3).start()

    def weights_3(i):
        for which in range(4):
            sibling(i, which, True).wait_recv()
        own(i).wait()

    for i in range(3):
        weights_0(i)

    def img_copy(dst, src):
        return remote(img, img_recv.at[src], img_ss.at[dst], img_rs.at[src], query=dst)

    for p in others:
        img_copy(p, me).start()

    def of(ref, p):
        return ref.at[pl.ds(p * SLOTS, SLOTS)]

    def q_copy(dst, src):
        return remote(of(qsend, dst), of(qrecv, src), q_ss.at[dst], q_rs.at[src], query=dst)

    def c_copy(dst, src):
        return remote(of(csend, dst), of(crecv, src), c_ss.at[dst], c_rs.at[src], query=dst)

    for k, p in enumerate(peers):
        for s in range(SLOTS):
            qsend[p * SLOTS + s] = qpk[idx[0, p * SLOTS + s]]
        if k:
            q_copy(p, me).start()

    for copy in loads[2:]:
        copy.wait()
    wkvx[192:256] = wkvx[128:192]
    wkvx[448:512] = wkvx[384:448]

    @pl.loop(0, 4)
    def _(i):
        rows = patches[pl.ds(i * 64, 64)].reshape(512, VIS)
        result = times(rows, wkvx[...])
        for c in range(4):
            both[c, pl.ds(i * 512, 512)] = result[:, c * 128 : c * 128 + 128]

    result = times(patches[256], wkvx[...])
    for c in range(4):
        both[c, 2048:2056] = result[:, c * 128 : c * 128 + 128]

    @pl.loop(0, IMAGES)
    def _(i):
        pad = jnp.zeros((KEYS - 256, 256), bf16)
        keys[i, 256:KEYS] = pad
        values[i, 256:KEYS] = pad
        for c in range(4):
            ref = keys if c < 2 else values
            part = both[c, pl.ds(i, PATCH, stride=IMAGES)].astype(bf16)
            ref[i, 0:PATCH, (c % 2) * 128 : (c % 2) * 128 + 128] = part

    img_recv[me] = img[...]

    for p in others:
        img_copy(p, p).wait_recv()

    to_scalars = pltpu.make_async_copy(img_recv, img_s, img_sem)
    to_scalars.start()
    to_scalars.wait()

    first_mask = low.astype(f32).astype(bf16)
    second_mask = (1 - low.astype(f32)).astype(bf16)
    column = lax.broadcasted_iota(jnp.int32, (1, KEYS), 1)

    factor = 0.125 * 1.4426950408889634

    def attend(slots, images):
        scores, weights, context, packed = [], [], [], []
        for slot, image in zip(slots, images):
            rows = qrecv[slot]
            a, b = rows[0:32], rows[32:48]
            top = jnp.concatenate([a * first_mask, a * second_mask, jnp.zeros((32, 128), bf16)], axis=0)
            bottom = jnp.concatenate([jnp.zeros((64, 128), bf16), b * first_mask, b * second_mask], axis=0)
            scores.append(times(jnp.concatenate([top, bottom], axis=1), keys[image]))
        for s in scores:
            s = jnp.where(column < PATCH, s, -jnp.inf)
            e = jnp.exp2((s - jnp.max(s, axis=1, keepdims=True)) * factor)
            weights.append((e * (1.0 / jnp.sum(e, axis=1, keepdims=True))).astype(bf16))
        for w, image in zip(weights, images):
            context.append(jnp.dot(w, values[image], preferred_element_type=f32))
        for c in context:
            c01 = jnp.where(low, c[0:32, :128], c[32:64, :128])
            c2 = jnp.where(low, c[64:80, 128:], c[80:96, 128:])
            packed.append(jnp.concatenate([c01, c2], axis=0).astype(bf16))
        return packed

    qrecv[pl.ds(me * SLOTS, SLOTS)] = qsend[pl.ds(me * SLOTS, SLOTS)]

    @pl.loop(0, GROUPS // NX)
    def _(n):
        four = [peer(n * NX + i) for i in range(NX)]
        for i, p in enumerate(four):
            if i:
                q_copy(p, p).wait_recv()
            else:
                pl.when(n > 0)(q_copy(p, p).wait_recv)
        for i in range(3):

            @pl.when(n == GROUPS // NX - 3 + i)
            def _():
                weights_1(i)

        slots = [p * SLOTS + s for p in four for s in range(SLOTS)]
        images = [img_s[p, 0, me * SLOTS + s] for p in four for s in range(SLOTS)]
        for slot, rows in zip(slots, attend(slots, images)):
            csend[slot] = rows
        for i, p in enumerate(four):
            if i:
                c_copy(p, me).start()
            else:
                pl.when(n > 0)(c_copy(p, me).start)

    crecv[pl.ds(me * SLOTS, SLOTS)] = csend[pl.ds(me * SLOTS, SLOTS)]

    for p in others:
        img_copy(p, p).wait_send()
        q_copy(p, p).wait_send()
        c_copy(p, p).wait_recv()

    def y_copy(dst, src):
        return remote(ysend.at[dst], yrecv.at[src], y_ss.at[dst], y_rs.at[src], tensor=dst)

    for k in (2, 1, 3):
        t = y_peer(k)
        for j in range(8):
            ysend[t, j] = crecv[idx[1, t * 8 + j]]
        y_copy(t, ty).start()
    for j in range(8):
        yrecv[ty, j] = crecv[idx[1, ty * 8 + j]]

    for p in others:
        c_copy(p, p).wait_send()

    for i in range(3):
        weights_2(i)
    weights_3(0)
    for t in range(TENSOR):
        wout[t, 192:256] = wout[t, 128:192]
    def norm(v):
        mean = jnp.mean(v, axis=-1, keepdims=True)
        squares = jnp.mean(v * v, axis=-1, keepdims=True)
        return (v - mean) * lax.rsqrt(squares - mean * mean + EPSILON)

    total = states[pl.ds(ty * 8, 8)].reshape(ROWS, D).astype(f32)
    for k in (0, 1, 3, 2):
        t = y_peer(k)
        if k:
            y_copy(t, t).wait_recv()
        c = yrecv[t]
        b = c[:, 32:]
        second = jnp.concatenate([b * first_mask[None], b * second_mask[None]], axis=1)
        rows = jnp.concatenate([c[:, :32], second], axis=2).reshape(ROWS, 256)
        total = total + jnp.dot(rows, wout[t], preferred_element_type=f32)
    first_norm = norm(total).astype(bf16)

    weights_3(1)
    weights_3(2)
    total = first_norm.astype(f32)

    def up(t):
        return jnp.dot(first_norm, win[t], preferred_element_type=f32)

    later = up(0)
    for t in range(TENSOR):
        now = later
        if t < TENSOR - 1:
            later = up(t + 1)
        hidden = (0.5 * now * (1.0 + lax.erf(now * 0.7071067811865476))).astype(bf16)
        total = total + jnp.dot(hidden, wdn[t], preferred_element_type=f32)
    score = jnp.sum(norm(total) * match_ref[...].astype(f32).reshape(1, D), axis=-1, keepdims=True)
    score = jnp.mean(score.reshape(8, NQ, 1), axis=1)

    lane = lax.broadcasted_iota(jnp.int32, (8, 128), 1)
    pair = lax.broadcasted_iota(jnp.int32, (8, 128), 0) + (core * PAIRS + ty * 8)
    row = jnp.sum(jnp.where(lane == pair, score, 0.0), axis=0, keepdims=True)
    fsend[...] = row
    frecv[core, ty] = row
    group = [(c, k) for c in (0, 1) for k in range(TENSOR) if c or k]

    def f_copy(c, k, receive=False):
        device = {"owner": lax.rem(core + c, 2), "tensor": y_peer(k)}
        at = (device["owner"], device["tensor"]) if receive else (core, ty)
        return remote(fsend, frecv.at[at], f_ss.at[c, k], f_rs.at[at], **device)

    for c, k in reversed(group):
        f_copy(c, k).start()
    for c, k in group:
        f_copy(c, k, True).wait_recv()
    row = jnp.sum(frecv[...].reshape(2 * TENSOR, 128), axis=0, keepdims=True)
    valid = lax.broadcasted_iota(jnp.int32, (1, 128), 1) < 2 * PAIRS
    partition = jnp.sum(jnp.where(valid, jnp.exp(row), 0.0), axis=1, keepdims=True)
    row = row - jnp.log(partition)
    row = jnp.where(core == 0, row, pltpu.roll(row, 128 - PAIRS, 1))
    osend[...] = row
    orecv[me] = row

    def o_copy(dst, src):
        return remote(osend, orecv.at[src], o_ss.at[dst], o_rs.at[src], query=dst)

    for p in reversed(others):
        o_copy(p, me).start()

    for k in range(1, TENSOR):
        t = y_peer(k)
        y_copy(t, t).wait_send()
    for c, k in group:
        f_copy(c, k).wait_send()
    for i in range(3):
        first_hop(i, True).wait_send()
        first_hop(i, False).wait_send()
        second_hop(i, True).wait_send()
        second_hop(i, False).wait_send()
        for which in range(4):
            sibling(i, which).wait_send()
    for p in others:
        o_copy(p, p).wait_send()

    for p in others:
        o_copy(p, p).wait_recv()

    out_ref[...] = orecv[...].reshape(GROUPS, 128)[:, :PAIRS]


def body(
    patches, states, pair_source, pair_image, w_query, w_key, w_value, w_out, w_in, w_down, w_match
):
    vmem = pl.BlockSpec(memory_space=pltpu.VMEM)
    hbm = pl.BlockSpec(memory_space=pl.ANY)
    dma = pltpu.SemaphoreType.DMA
    return pl.pallas_call(
        kernel,
        out_shape=jax.ShapeDtypeStruct((GROUPS, PAIRS), f32),
        in_specs=[hbm] * 11,
        out_specs=vmem,
        scratch_shapes=[
            pltpu.VMEM((1, PAIRS), jnp.int32),
            pltpu.VMEM((1, PAIRS), jnp.int32),
            pltpu.VMEM((D,), bf16),
            pltpu.VMEM((PAIRS, NQ, D), bf16),
            pltpu.VMEM((PATCH, IMAGES, VIS), bf16),
            pltpu.VMEM((256, D), bf16),
            pltpu.VMEM((512, VIS), bf16),
            pltpu.VMEM((4, (PATCH + 7) * IMAGES, 128), f32),
            pltpu.VMEM((1, 128), jnp.int32),
            pltpu.VMEM((2, 128), jnp.int32),
            pltpu.SMEM((2, 128), jnp.int32),
            pltpu.VMEM((PAIRS, PACK, 128), bf16),
            pltpu.VMEM((GROUPS * SLOTS, PACK, 128), bf16),
            pltpu.VMEM((GROUPS * SLOTS, PACK, 128), bf16),
            pltpu.VMEM((GROUPS * SLOTS, PACK, 128), bf16),
            pltpu.VMEM((GROUPS * SLOTS, PACK, 128), bf16),
            pltpu.VMEM((IMAGES, KEYS, 256), bf16),
            pltpu.VMEM((IMAGES, KEYS, 256), bf16),
            pltpu.VMEM((GROUPS, 1, 128), jnp.int32),
            pltpu.SMEM((GROUPS, 1, 128), jnp.int32),
            pltpu.VMEM((TENSOR, 8, PACK, 128), bf16),
            pltpu.VMEM((TENSOR, 8, PACK, 128), bf16),
            pltpu.VMEM((TENSOR, 256, D), bf16),
            pltpu.VMEM((TENSOR, D, D), bf16),
            pltpu.VMEM((TENSOR, D, D), bf16),
            pltpu.VMEM((1, 128), f32),
            pltpu.VMEM((2, TENSOR, 1, 128), f32),
            pltpu.VMEM((1, 128), f32),
            pltpu.VMEM((GROUPS, 1, 128), f32),
            dma((3,)), dma((5,)),
            dma((GROUPS,)), dma((GROUPS,)),
            dma((GROUPS,)), dma((GROUPS,)),
            dma((GROUPS,)), dma((GROUPS,)),
            dma((TENSOR,)), dma((TENSOR,)),
            dma((3,)), dma((3, 8)), dma((3, 8)),
            dma((2, TENSOR)), dma((2, TENSOR)),
            dma((GROUPS,)), dma((GROUPS,)),
            dma, dma,
        ],
        compiler_params=pltpu.CompilerParams(
            collective_id=0, has_side_effects=True, vmem_limit_bytes=56 * 1024 * 1024
        ),
    )(
        pair_source.reshape(1, PAIRS), pair_image.reshape(1, PAIRS), w_match, states,
        jnp.transpose(patches[0, 0], (1, 0, 2)), w_query.T, w_key.T, w_value.T, w_out, w_in, w_down,
    )


def solution(mesh):
    placed = (
        P("query", "owner", None, None, None),
        P(("query", "owner"), None, None),
        P(("query", "owner"), None),
        P(("query", "owner")),
        P(None, "tensor"),
        P(None, "tensor"),
        P(None, "tensor"),
        P("tensor", None),
        P(None, "tensor"),
        P("tensor", None),
        P(),
    )
    return jax.shard_map(
        body, mesh=mesh, in_specs=placed, out_specs=P(None, "owner"), check_vma=False
    )
```
